512 devices in a mesh: gx: 32 (over z, core), gy: 4 (over x), gz: 4 (over y).
Axes of the slice: x: 4, y: 4, z: 16, core: 2. Of those that a mesh axis runs over, the one named last changes fastest.
Arguments:
- positions: float32 [32, 4, 4, 3, 512], P('gx', 'gy', 'gz'), may hold values from 0 to 1.5
- species: int32 [32, 4, 4, 512], P('gx', 'gy', 'gz'), may hold values from 0 to 2
- plan: int32 [32, 4, 4, 4], P('gx', 'gy', 'gz'), may hold values from 0 to 2, as said below
- pair_centre: int32 [32, 4, 4, 512], P('gx', 'gy', 'gz'), may hold values from 0 to 767, as said below
- pair_neighbour: int32 [32, 4, 4, 512], P('gx', 'gy', 'gz'), may hold values from 0 to 20735, as said below
- pair_blocks: int32 [32, 4, 4], P('gx', 'gy', 'gz'), may hold values from 1 to 4
- w_in: bfloat16 [256, 14], replicated, may hold values from -1.5 to 1.5
- w_hidden: bfloat16 [256, 256], replicated, may hold values from -0.375 to 0.375
- w_env: bfloat16 [2, 64, 256], replicated, may hold values from -0.375 to 0.375
- w_latent: bfloat16 [2, 256, 320], replicated, may hold values from -0.3125 to 0.3125
- w_out: bfloat16 [256], replicated, may hold values from -0.375 to 0.375
Outputs:
- forces: float32 [32, 4, 4, 3, 768], P('gx', 'gy', 'gz')
- domain_energy: float32 [32, 4, 4], P('gx', 'gy', 'gz')
The draws below stay inside these ranges and needn't reach their ends.
Inputs may be any that keep to these rules, and one draw needn't show every extreme that they name: Each domain sends at most 1 block with plan 1 and at most 1 with plan 2; some domain sends 1 each way. `pair_centre`: live pairs name slots of the layout that hold an atom; padded pairs may name any slot. `pair_neighbour`: live pairs name a slot of the extended array that holds an atom and is not the pair's centre; padded pairs may name any slot.
All inputs are finite; a program needn't handle non-finite values.
Results may differ from the reference program's by a relative error of at most 0.039.
Values sent between devices are 32-bit elements; how exact they have to be, the bound alone decides.
A program may use at most 64 MiB of HBM per device.

```python
import jax
import jax.numpy as jnp
from jax import lax

CH = 256
MULT = 64
NBASIS = 8
NSPEC = 3
LAYERS = 2
ATOM_BLK = 128
PAIR_BLK = 128
CAP = 1
NB = 4
NPB = 4
ATOMS_DEV = 512
SLOTS = 768
PAIRS = 512
N_GX = 32
N_GY = 4
N_GZ = 4


def draw_everything(key):
    keys = jax.random.split(key, 6)
    grid_shape = (N_GX, N_GY, N_GZ)
    domains = N_GX * N_GY * N_GZ
    uppers = jax.random.randint(keys[0], grid_shape, 0, CAP + 1).at[0, 0, 0].set(CAP)
    lowers = jax.random.randint(keys[1], grid_shape, 0, CAP + 1).at[0, 0, 0].set(CAP)
    scores = jax.random.randint(keys[2], grid_shape + (NB,), 0, 1 << 20) * NB + jnp.arange(NB)
    ranking = jnp.argsort(jnp.argsort(scores, axis=-1), axis=-1)
    plan = jnp.where(ranking < uppers[..., None], 1, jnp.where(ranking < (uppers + lowers)[..., None], 2, 0)).astype(jnp.int32)
    slot_ids = jnp.arange(CAP)
    lower_live = slot_ids < jnp.roll(uppers, 1, axis=0)[..., None]
    upper_live = slot_ids < jnp.roll(lowers, -1, axis=0)[..., None]
    block_live = jnp.concatenate([lower_live, plan == 0, upper_live], -1).astype(jnp.int32)
    slot_live = jnp.repeat(block_live, ATOM_BLK, axis=-1)
    ghost_live = []
    for offset_index in range(27):
        shift_x = offset_index // 9 - 1
        shift_y = offset_index // 3 % 3 - 1
        shift_z = offset_index % 3 - 1
        ghost_live.append(jnp.roll(slot_live, (-shift_x, -shift_y, -shift_z), axis=(0, 1, 2)))
    ext_live = jnp.stack(ghost_live, 3).reshape(domains, 27 * SLOTS)
    local_live = slot_live.reshape(domains, SLOTS)
    cum_local = jnp.cumsum(local_live, -1)
    cum_ext = jnp.cumsum(ext_live, -1)

    def locate(cumulative, targets):
        return jnp.searchsorted(cumulative, targets, side='right').astype(jnp.int32)
    centre_draw = jax.random.randint(keys[3], (domains, PAIRS), 0, cum_local[:, -1:])
    centre = jax.vmap(locate)(cum_local, centre_draw)
    self_rank = jnp.take_along_axis(cum_ext, centre + 13 * SLOTS, 1) - 1
    neighbour_draw = jax.random.randint(keys[4], (domains, PAIRS), 0, cum_ext[:, -1:] - 1)
    neighbour_draw = neighbour_draw + (neighbour_draw >= self_rank).astype(jnp.int32)
    neighbour = jax.vmap(locate)(cum_ext, neighbour_draw)
    blocks = jax.random.randint(keys[5], (domains,), 1, NPB + 1).at[0].set(NPB).at[1].set(1)
    centre = centre.at[1, PAIRS - 1].set(SLOTS - 1).at[1, PAIRS - 2].set(0)
    neighbour = neighbour.at[1, PAIRS - 1].set(27 * SLOTS - 1).at[1, PAIRS - 2].set(0)
    return (plan, centre.reshape(grid_shape + (PAIRS,)).astype(jnp.int32), neighbour.reshape(grid_shape + (PAIRS,)).astype(jnp.int32), blocks.reshape(grid_shape).astype(jnp.int32))


def draw_plan(key, part):
    return draw_everything(key)[0]


def draw_pair_centre(key, part):
    return draw_everything(key)[1]


def draw_pair_neighbour(key, part):
    return draw_everything(key)[2]


def draw_pair_blocks(key, part):
    return draw_everything(key)[3]


def with_ends(result, stream_key, low, largest):
    longest = result.shape.index(max(result.shape))
    spots = []
    for shift in (0, 1):
        where = [jax.random.randint(jax.random.fold_in(stream_key, axis), (), 0, length) for axis, length in enumerate(result.shape)]
        where[longest] = (where[longest] + shift) % result.shape[longest]
        spots.append(tuple(where))
    return result.at[spots[0]].set(low).at[spots[1]].set(largest)


def block_levels(stream_key, dims, cuts, low, largest):
    def one(dim, blocks):
        heights = jax.random.uniform(jax.random.fold_in(jax.random.fold_in(stream_key, 6), dim), (blocks,), jnp.float32, low / len(cuts), largest / len(cuts))
        return jnp.repeat(jnp.exp(heights), dims[dim] // blocks).reshape((-1,) + (1,) * (len(dims) - dim - 1))

    level = one(*cuts[0])
    for cut in cuts[1:]:
        level = level * one(*cut)
    return level


def noise(key, shape, deviation, limit, held_as=jnp.bfloat16):
    entries = deviation * jax.random.normal(key, shape, jnp.float32)
    return jnp.clip(entries, min=-limit, max=limit).astype(held_as)


def setup_inputs(seed: int = 0) -> dict:
    streams_of = jax.random.split(jax.random.key(seed), 12)
    return {
        "positions": jnp.clip(1.5 * jax.random.uniform(streams_of[0], (N_GX, N_GY, N_GZ, 3, ATOMS_DEV), jnp.float32) ** block_levels(streams_of[0], (N_GX, N_GY, N_GZ, 3, ATOMS_DEV), ((0, 32), (1, 4), (2, 4)), -0.2, 0.2), 0.0, 1.5),
        "species": with_ends(jax.random.randint(streams_of[1], (N_GX, N_GY, N_GZ, ATOMS_DEV), 0, NSPEC), jax.random.fold_in(streams_of[1], 1), 0, NSPEC - 1).astype(jnp.int32),
        "plan": draw_plan(jax.random.fold_in(streams_of[11], 71), 0),
        "pair_centre": draw_pair_centre(jax.random.fold_in(streams_of[11], 71), 0),
        "pair_neighbour": draw_pair_neighbour(jax.random.fold_in(streams_of[11], 71), 0),
        "pair_blocks": draw_pair_blocks(jax.random.fold_in(streams_of[11], 71), 0),
        "w_in": noise(streams_of[6], (CH, NBASIS + 2 * NSPEC), (NBASIS + 2 * NSPEC) ** -0.5, 1.5),
        "w_hidden": noise(streams_of[7], (CH, CH), CH ** -0.5, 0.375),
        "w_env": noise(streams_of[8], (LAYERS, MULT, CH), CH ** -0.5, 0.375),
        "w_latent": noise(streams_of[9], (LAYERS, CH, CH + MULT), (CH + MULT) ** -0.5, 0.3125),
        "w_out": noise(streams_of[10], (CH,), CH ** -0.5, 0.375),
    }


edge_length = 1.5
cutoff = 9.0
softening = 0.5
env_scale = 0.5

def offset_table():
    offset_ids = jnp.arange(27)
    return jnp.stack([offset_ids // 9 - 1, offset_ids // 3 % 3 - 1, offset_ids % 3 - 1], 1).astype(jnp.float32)

def pack_blocks(block_data, chosen_mask, x_shift):
    chosen = chosen_mask.astype(jnp.int32)
    ranking = jnp.cumsum(chosen, axis=-1) - 1
    slot_ids = jnp.arange(CAP, dtype=jnp.int32)
    chosen_slots = ((ranking[..., None, :] == slot_ids[:, None]) & (chosen[..., None, :] == 1)).astype(jnp.float32)
    packed = jnp.einsum('...kb,...bcs->...kcs', chosen_slots, block_data, precision=lax.Precision.HIGHEST)
    filled = lax.optimization_barrier(jnp.sum(chosen_slots, -1))
    first_channel = (jnp.arange(4) == 0).astype(jnp.float32)
    return packed + x_shift * filled[..., :, None, None] * first_channel[:, None]

def pair_energy(ext_pos, ext_kind, centre, neighbour, live_pairs, w_in, w_hidden, w_env, w_latent, w_out):
    slot_count = ext_pos.shape[2]
    pair_total = centre.shape[0]
    flat_pos = jnp.transpose(ext_pos, (1, 0, 2)).reshape(3, 27 * slot_count)
    flat_kind = ext_kind.reshape(27 * slot_count)
    centre_ext = centre + 13 * slot_count
    displacement = flat_pos[:, neighbour] - flat_pos[:, centre_ext]
    distance = jnp.sqrt(lax.optimization_barrier(jnp.sum(displacement * displacement, 0)) + softening * softening)
    direction = displacement / distance[None]
    scaled = distance / cutoff
    envelope = (1.0 - scaled * scaled) ** 2
    basis_orders = jnp.arange(1, NBASIS + 1).astype(jnp.float32)
    radial_basis = jnp.sin(basis_orders[:, None] * jnp.pi * scaled[None]) / distance[None] * envelope[None]
    species_ids = jnp.arange(NSPEC).astype(jnp.float32)
    centre_hot = (flat_kind[centre_ext][None] == species_ids[:, None]).astype(jnp.float32)
    neighbour_hot = (flat_kind[neighbour][None] == species_ids[:, None]).astype(jnp.float32)
    features = jnp.concatenate([radial_basis, centre_hot, neighbour_hot], 0).astype(jnp.bfloat16)
    first_hidden = jax.nn.silu(jnp.dot(w_in, features, preferred_element_type=jnp.float32)).astype(jnp.bfloat16)
    latent = jax.nn.silu(jnp.dot(w_hidden, first_hidden, preferred_element_type=jnp.float32)) * envelope[None]
    harmonics = jnp.concatenate([jnp.ones((1, pair_total), jnp.float32), direction], 0)
    for layer_index in range(LAYERS):
        latent_half = latent.astype(jnp.bfloat16)
        env_weights = jnp.dot(w_env[layer_index], latent_half, preferred_element_type=jnp.float32) * live_pairs[None]
        env_terms = (harmonics[:, None, :] * env_weights[None]).reshape(4 * MULT, pair_total)
        environment = jnp.zeros((4 * MULT, slot_count), jnp.float32).at[:, centre].add(env_terms)
        centre_env = environment[:, centre].reshape(4, MULT, pair_total)
        invariant = (env_scale * env_weights * lax.optimization_barrier(jnp.sum(harmonics[:, None, :] * centre_env, 0))).astype(jnp.bfloat16)
        combined = jnp.concatenate([latent_half, invariant], 0)
        latent = latent + jax.nn.silu(jnp.dot(w_latent[layer_index], combined, preferred_element_type=jnp.float32))
    pair_values = jnp.dot(w_out, latent.astype(jnp.bfloat16), preferred_element_type=jnp.float32)
    return jnp.sum(pair_values * live_pairs)

def reference(positions, species, plan, pair_centre, pair_neighbour, pair_blocks, w_in, w_hidden, w_env, w_latent, w_out):
    grid_shape = (N_GX, N_GY, N_GZ)
    coords = positions.reshape(grid_shape + (3, NB, ATOM_BLK)).transpose(0, 1, 2, 4, 3, 5)
    kind_rows = (species.astype(jnp.float32) + 1.0).reshape(grid_shape + (NB, 1, ATOM_BLK))
    block_data = jnp.concatenate([coords, kind_rows], 4)
    packed_up = pack_blocks(block_data, plan == 1, -edge_length)
    packed_down = pack_blocks(block_data, plan == 2, edge_length)
    staying = (plan == 0).astype(jnp.float32)[..., None, None] * block_data
    arranged = jnp.concatenate([jnp.roll(packed_up, 1, axis=0), staying, jnp.roll(packed_down, -1, axis=0)], 3)
    layout = arranged.transpose(0, 1, 2, 4, 3, 5).reshape(grid_shape + (4, SLOTS))
    offsets = offset_table()
    ghost_blocks = []
    for offset_index in range(27):
        shift_x = offset_index // 9 - 1
        shift_y = offset_index // 3 % 3 - 1
        shift_z = offset_index % 3 - 1
        ghost_blocks.append(jnp.roll(layout, (-shift_x, -shift_y, -shift_z), axis=(0, 1, 2)))
    extended = jnp.stack(ghost_blocks, 3)
    domains = N_GX * N_GY * N_GZ
    ext_flat = extended.reshape(domains, 27, 4, SLOTS)

    def one_domain(domain_items):
        extended_block, centre, neighbour, blocks = domain_items
        ext_pos = extended_block[:, :3] + edge_length * offsets[:, :, None]
        ext_kind = extended_block[:, 3] - 1.0
        live_pairs = (jnp.arange(PAIRS) < blocks * PAIR_BLK).astype(jnp.float32)

        def energy_of(field_pos):
            return pair_energy(field_pos, ext_kind, centre, neighbour, live_pairs, w_in, w_hidden, w_env, w_latent, w_out)
        energy, pullback = jax.vjp(energy_of, ext_pos)
        return (energy, -pullback(jnp.ones((), jnp.float32))[0])
    energies, partial_value = lax.map(one_domain, (ext_flat, pair_centre.reshape(domains, PAIRS), pair_neighbour.reshape(domains, PAIRS), pair_blocks.reshape(domains)))
    partial_value = partial_value.reshape(grid_shape + (27, 3, SLOTS))
    forces = jnp.zeros(grid_shape + (3, SLOTS), jnp.float32)
    for offset_index in range(27):
        shift_x = offset_index // 9 - 1
        shift_y = offset_index // 3 % 3 - 1
        shift_z = offset_index % 3 - 1
        forces = forces + jnp.roll(partial_value[:, :, :, offset_index], (shift_x, shift_y, shift_z), axis=(0, 1, 2))
    return (forces, energies.reshape(grid_shape))
```

```python
import functools

import jax
import jax.numpy as jnp
from jax import lax
from jax.experimental import pallas as pl
from jax.experimental.pallas import tpu as pltpu
from jax.sharding import PartitionSpec as P

MESH = pl.DeviceIdType.MESH

CH = 256
MULT = 64
NBASIS = 8
NSPEC = 3
BLK = 128
NB = 4
PAIRS = 512
CHUNK = 256
CHUNKS = PAIRS // CHUNK

EDGE = 1.5
CUTOFF = 9.0
SOFT2 = 0.25

GROUP = 18
FIRST = {-2: 0, -1: 1, 0: 6, 1: 12, 2: 17}
SENT = {-2: (5, 1), -1: (1, 5), 0: (0, 6), 1: (0, 5), 2: (0, 1)}
ROWS = 9 * GROUP
PADDED = 176
OWN = 4 * GROUP + FIRST[0]

F32 = jnp.float32
BF16 = jnp.bfloat16


def dot(a, b):
    return lax.dot_general(a, b, (((1,), (0,)), ((), ())), preferred_element_type=F32)


def dot_tn(a, b):
    return lax.dot_general(a, b, (((0,), (0,)), ((), ())), preferred_element_type=F32)


def dot_nt(a, b):
    return lax.dot_general(a, b, (((1,), (1,)), ((), ())), preferred_element_type=F32)


def halves(x):
    high = x.astype(BF16)
    return high, (x - high.astype(F32)).astype(BF16)


def rows_of(shape):
    return lax.broadcasted_iota(jnp.int32, shape, 0)


def series(u, terms):
    total = jnp.full_like(u, terms[-1])
    for term in terms[-2::-1]:
        total = total * u + term
    return total


def sin_cos_half_turns(t):
    k = jnp.floor(t + 0.5)
    f = (t - k) * 3.14159265358979
    sign = 1.0 - 2.0 * (k - 2.0 * jnp.floor(0.5 * k))
    u = f * f
    sine = f * series(u, [1.0, -1 / 6, 1 / 120, -1 / 5040, 1 / 362880, -1 / 39916800, 1 / 6227020800])
    cosine = series(
        u, [1.0, -1 / 2, 1 / 24, -1 / 720, 1 / 40320, -1 / 3628800, 1 / 479001600, -1 / 87178291200]
    )
    return sign * sine, sign * cosine


def silu_parts(x):
    gate = 0.5 + 0.5 * jnp.tanh(0.5 * x)
    value = x * gate
    return value, gate + value * (1.0 - gate)


def kernel(
    sizes,
    pos_hbm, kind_hbm, plan_hbm, centre_hbm, neighbour_hbm, blocks_hbm,
    w_in_hbm, w_hidden_hbm, w_env_hbm, w_latent_hbm, w_out_hbm,
    forces_ref, energy_ref,
    pos, kind, plan, centre, neighbour, blocks,
    w_in_raw, w_hidden, w_env, w_latent_t, w_out,
    w_in_t, w_in, w_hidden_t, w_back, w_latent,
    mine, held, lane_neighbour, lane_centre, same,
    d1, d2, h2, latent, grad, inners, dz, env_w, env_a, stacked_a, stacked_b,
    partial, arrived,
    in_sems, send_sem, recv_sem, back_send_sem, back_recv_sem,
):
    place = [lax.axis_index(axis) for axis in ("gx", "gy", "gz")]

    def device(steps):
        return tuple(
            lax.rem(at + (step + size), size) if step else at
            for at, step, size in zip(place, steps, sizes)
        )

    far = [(a, b, c) for b in (-1, 0, 1) for c in (-1, 0, 1) for a in (-2, -1, 0, 1, 2)]
    far = [o for o in far if o != (0, 0, 0)]
    far.sort(key=lambda o: -(abs(o[0]) + abs(o[1]) + abs(o[2])))
    near = [o for o in far if abs(o[0]) < 2]

    pairs_in = [
        (pos_hbm.at[0, 0], pos),
        (kind_hbm.at[0, 0], kind),
        (plan_hbm.at[0, 0], plan),
        (centre_hbm.at[0, 0], centre),
        (neighbour_hbm.at[0, 0], neighbour),
        (blocks_hbm.at[0], blocks),
        (w_in_hbm, w_in_raw),
        (w_hidden_hbm, w_hidden),
        (w_env_hbm, w_env),
        (w_latent_hbm, w_latent_t),
        (w_out_hbm, w_out),
    ]
    loads = [
        pltpu.make_async_copy(source, target, in_sems.at[i])
        for i, (source, target) in enumerate(pairs_in)
    ]
    for load in loads:
        load.start()

    barrier = pltpu.get_barrier_semaphore()
    for offset in far:
        pl.semaphore_signal(barrier, inc=1, device_id=device(offset), device_id_type=MESH)

    for load in loads[:3]:
        load.wait()
    kind_rows = kind[...].astype(F32) + 1.0
    for b in range(NB):
        lanes_of = slice(b * BLK, (b + 1) * BLK)
        for c in range(3):
            mine[1 + b, c : c + 1] = pos[c, :, lanes_of]
        mine[1 + b, 3:4] = kind_rows[:, lanes_of]
    first_row = (rows_of((4, BLK)) == 0).astype(F32)
    for slot, move, shift in ((0, 1, -EDGE), (5, 2, EDGE)):
        packed = jnp.zeros((4, BLK), F32)
        for b in range(NB):
            chosen = jnp.where(plan[0, b] == move, 1.0, 0.0).astype(F32)
            packed = packed + chosen * (mine[1 + b] + shift * first_row)
        mine[slot] = packed
    held[OWN : OWN + 6] = mine[...]

    pl.semaphore_wait(barrier, len(far))
    for offset in far:
        a, b, c = offset
        start, count = SENT[a]
        where = (3 * (1 - b) + (1 - c)) * GROUP + FIRST[-a]
        pltpu.make_async_remote_copy(
            src_ref=mine.at[pl.ds(start, count)],
            dst_ref=held.at[pl.ds(where, count)],
            send_sem=send_sem,
            recv_sem=recv_sem,
            device_id=device(offset),
            device_id_type=MESH,
        ).start()

    for load in loads[3:]:
        load.wait()
    centre_row = centre[...]
    neighbour_row = neighbour[...]
    live = jnp.where(
        lax.broadcasted_iota(jnp.int32, (1, PAIRS), 1) < blocks[0, 0] * BLK, 1.0, 0.0
    ).astype(F32)
    centre_block = centre_row >> 7
    centre_lane = centre_row & 127
    block = neighbour_row >> 7
    neighbour_lane = neighbour_row & 127
    box = (block * 10923) >> 16
    k = block - 6 * box
    box_x = (box * 7282) >> 16
    box_yz = box - 9 * box_x
    box_y = (box_yz * 21846) >> 16
    box_z = box_yz - 3 * box_y

    def held_row(x, yz, k):
        up = jnp.where(x == 2, 6, x)
        down = jnp.where(x == 0, 11, 15 + x)
        return yz * GROUP + jnp.where(k == 0, up, jnp.where(k == 5, down, 1 + 5 * x + k))

    neighbour_held = held_row(box_x, box_yz, k)
    centre_held = held_row(jnp.ones_like(centre_block), jnp.zeros_like(centre_block), centre_block)
    lanes = rows_of((BLK, PAIRS))
    hot = jnp.where(lanes == neighbour_lane, 1.0, 0.0).astype(BF16)
    lane_neighbour[:BLK] = hot
    lane_neighbour[BLK:] = hot
    hot = jnp.where(lanes == centre_lane, 1.0, 0.0).astype(BF16)
    lane_centre[:BLK] = hot
    lane_centre[BLK:] = hot
    centre_column = jnp.transpose(
        jnp.broadcast_to(centre_row.astype(F32), (8, PAIRS)), (1, 0)
    )[:, 0:1]
    same[...] = jnp.where(centre_column == centre_row.astype(F32), 1.0, 0.0).astype(F32)

    w_hidden_t[...] = jnp.transpose(w_hidden[...].astype(F32), (1, 0)).astype(BF16)
    for l in range(2):
        padding = jnp.zeros((BLK - MULT, CH), F32)
        rows = jnp.concatenate([w_env[l].astype(F32), padding], axis=0)
        w_back[l, :, :CH] = w_latent_t[l, :CH]
        w_back[l, :, CH:] = jnp.transpose(rows, (1, 0)).astype(BF16)
        rows = jnp.concatenate([w_latent_t[l].astype(F32), padding], axis=0)
        w_latent[l] = jnp.transpose(rows, (1, 0)).astype(BF16)
    fewer = NBASIS + 2 * NSPEC
    rows = jnp.concatenate([w_in_raw[...].astype(F32), jnp.zeros((BLK - fewer, CH), F32)], axis=0)
    w_in_t[...] = rows[:16].astype(BF16)
    w_in[...] = jnp.transpose(rows, (1, 0)).astype(BF16)
    no_rows = jnp.zeros((BLK - MULT, CHUNK), BF16)
    out_row = jnp.concatenate([w_out[0:1], w_out[1:2]], axis=1)
    out_column = jnp.transpose(jnp.broadcast_to(out_row.astype(F32), (8, CH)), (1, 0))[:, 0:1]
    grad[...] = out_column * live

    incoming = ROWS - 6
    pltpu.make_async_copy(
        held.at[pl.ds(0, incoming)], held.at[pl.ds(0, incoming)], recv_sem
    ).wait()

    neighbour_mask = rows_of((ROWS, PAIRS)) == neighbour_held
    centre_mask = rows_of((GROUP, PAIRS)) == centre_held
    near_rows = []
    own_rows = []
    for c in range(4):
        table = held[:, c, :]
        high, low = halves(table)
        both = jnp.concatenate([high, low], axis=1)
        found = dot(both, lane_neighbour[...])
        near_rows.append(jnp.sum(jnp.where(neighbour_mask, found, 0.0), axis=0, keepdims=True))
        table = held[4 * GROUP : 5 * GROUP, c, :]
        high, low = halves(table)
        both = jnp.concatenate([high, low], axis=1)
        found = dot(both, lane_centre[...])
        own_rows.append(jnp.sum(jnp.where(centre_mask, found, 0.0), axis=0, keepdims=True))

    shifts = [EDGE * (v.astype(F32) - 1.0) for v in (box_x, box_y, box_z)]
    gap = [near_rows[c] + shifts[c] - own_rows[c] for c in range(3)]
    square = gap[0] * gap[0] + gap[1] * gap[1] + gap[2] * gap[2]
    inverse = lax.rsqrt(square + SOFT2)
    distance = (square + SOFT2) * inverse
    way = [g * inverse for g in gap]
    scaled = distance * (1.0 / CUTOFF)
    falling = 1.0 - scaled * scaled
    envelope = falling * falling
    orders = (rows_of((NBASIS, PAIRS)) + 1).astype(F32)
    sine, cosine = sin_cos_half_turns(orders * scaled)
    over = sine * inverse
    radial = over * envelope
    r8 = rows_of((8, PAIRS)).astype(F32)
    own_kind = own_rows[3] - 1.0
    near_kind = near_rows[3] - 1.0
    one_hots = jnp.where(
        r8 < NSPEC,
        jnp.where(r8 == own_kind, 1.0, 0.0),
        jnp.where(r8 - NSPEC == near_kind, jnp.where(r8 < 2 * NSPEC, 1.0, 0.0), 0.0),
    )
    features = jnp.concatenate(
        [radial, one_hots, jnp.zeros((BLK - 16, PAIRS), F32)], axis=0
    ).astype(BF16)

    y4 = jnp.concatenate([jnp.ones_like(distance)] + way, axis=0)
    y_high, y_low = halves(y4)
    none = jnp.zeros_like(y_high)
    products = dot_tn(
        jnp.concatenate([y_high, y_high, y_low, none], axis=0).astype(F32),
        jnp.concatenate([y_high, y_low, y_high, none], axis=0).astype(F32),
    )
    g_matrix = (same[...] * products).astype(BF16)

    spans = [slice(j * CHUNK, (j + 1) * CHUNK) for j in range(CHUNKS)]

    before = []
    for s in spans:
        value, slope = silu_parts(dot(w_in[...], features[:, s]))
        d1[:, s] = slope
        value, slope = silu_parts(dot(w_hidden[...], value.astype(BF16)))
        d2[:, s] = slope
        h2[:, s] = value
        latent[:, s] = value * envelope[:, s]
    for l in range(2):
        for j, s in enumerate(spans):
            half = latent[:, s].astype(BF16)
            env_w[l, :, s] = dot(w_env[l], half) * live[:, s]
            dz[l, :, s] = dot(w_latent[l, :, :CH], half)
        weights_half = env_w[l].astype(BF16)
        for j, s in enumerate(spans):
            gathered = dot(weights_half, g_matrix[:, s])
            env_a[l, :, s] = gathered
            invariant = (0.5 * env_w[l, :, s] * gathered).astype(BF16)
            value, slope = silu_parts(dz[l, :, s] + dot(w_latent[l, :, CH:], jnp.concatenate([invariant, no_rows], axis=0)))
            dz[l, :, s] = slope
            latent[:, s] = latent[:, s] + value
    energy = jnp.zeros((1, 1), F32)
    for s in spans:
        values = dot(out_row, latent[:, s].astype(BF16))
        energy = energy + jnp.sum(values * live[:, s], axis=1, keepdims=True)
    energy_ref[0] = energy

    for l in (1, 0):
        for s in spans:
            inner = (grad[:, s] * dz[l, :, s]).astype(BF16)
            inners[:, s] = inner
            d_invariant = 0.5 * dot(w_latent_t[l, CH:], inner)
            stacked_a[(2 + l) * MULT : (3 + l) * MULT, s] = d_invariant * env_w[l, :, s]
            env_a[l, :, s] = d_invariant * env_a[l, :, s]
        d_gathered = stacked_a[(2 + l) * MULT : (3 + l) * MULT, :].astype(BF16)
        for s in spans:
            d_weights = (env_a[l, :, s] + dot(d_gathered, g_matrix[:, s])) * live[:, s]
            both = jnp.concatenate([inners[:, s], d_weights.astype(BF16), no_rows], axis=0)
            grad[:, s] = grad[:, s] + dot(w_back[l], both)
    d_radial = []
    d_envelope = []
    for s in spans:
        d_latent = grad[:, s]
        d_envelope.append(jnp.sum(d_latent * h2[:, s], axis=0, keepdims=True))
        inner = (d_latent * envelope[:, s] * d2[:, s]).astype(BF16)
        inner = (dot(w_hidden_t[...], inner) * d1[:, s]).astype(BF16)
        d_radial.append(dot(w_in_t[...], inner)[:NBASIS])
    d_radial = jnp.concatenate(d_radial, axis=1)
    d_envelope = jnp.concatenate(d_envelope, axis=1)

    for l in range(2):
        stacked_a[l * MULT : (l + 1) * MULT, :] = env_w[l]
        stacked_b[l * MULT : (l + 1) * MULT, :] = stacked_a[(2 + l) * MULT : (3 + l) * MULT, :].astype(BF16)
        stacked_b[(2 + l) * MULT : (3 + l) * MULT, :] = env_w[l].astype(BF16)
    left = jnp.transpose(stacked_a[...], (1, 0)).astype(BF16)
    d_products = (same[...] * dot(left, stacked_b[...])).astype(BF16)
    d_y = dot(y_high, d_products)
    d_way = [d_y[1 + c : 2 + c] for c in range(3)]

    slope_envelope = falling * scaled * (-4.0 / CUTOFF)
    d_envelope = d_envelope + jnp.sum(d_radial * over, axis=0, keepdims=True)
    d_over = d_radial * envelope
    turning = cosine * orders * (3.14159265358979 / CUTOFF) - over
    d_distance = (
        d_envelope * slope_envelope
        + inverse * jnp.sum(d_over * turning, axis=0, keepdims=True)
        - inverse * (d_way[0] * way[0] + d_way[1] * way[1] + d_way[2] * way[2])
    )
    gradient = [d_way[c] * inverse + d_distance * way[c] for c in range(3)]

    g8 = jnp.concatenate(gradient + [jnp.zeros((5, PAIRS), F32)], axis=0)
    g_high = g8.astype(BF16).astype(F32)
    g_low = g8 - g_high
    block_mask = rows_of((PADDED, PAIRS)) == block
    for c in range(3):
        high, low = -g_high[c : c + 1], -g_low[c : c + 1]
        spread = jnp.concatenate(
            [
                jnp.where(block_mask, high, 0.0).astype(BF16),
                jnp.where(block_mask, low, 0.0).astype(BF16),
            ],
            axis=0,
        )
        both = dot_nt(spread, lane_neighbour[:BLK])
        partial[:, c, :] = both[:ROWS] + both[PADDED : PADDED + ROWS]
    for offset in near:
        a, b, c = offset
        at = 9 * (a + 1) + 3 * (b + 1) + (c + 1)
        pltpu.make_async_remote_copy(
            src_ref=partial.at[pl.ds(6 * at, 6)],
            dst_ref=arrived.at[pl.ds(6 * at, 6)],
            send_sem=back_send_sem,
            recv_sem=back_recv_sem,
            device_id=device(offset),
            device_id_type=MESH,
        ).start()
    arrived[6 * 13 : 6 * 14] = partial[6 * 13 : 6 * 14]
    own_mask = rows_of((8, PAIRS)) == centre_block
    own_parts = []
    for c in range(3):
        high, low = g_high[c : c + 1], g_low[c : c + 1]
        spread = jnp.concatenate(
            [
                jnp.where(own_mask, high, 0.0),
                jnp.where(own_mask, low, 0.0),
            ],
            axis=0,
        ).astype(BF16)
        both = dot_nt(spread, lane_centre[:BLK])
        own_parts.append(both[:8] + both[8:])
    pltpu.make_async_copy(
        arrived.at[pl.ds(0, 6 * 26)], arrived.at[pl.ds(0, 6 * 26)], back_recv_sem
    ).wait()
    for s in range(6):
        total = arrived[s]
        for o in range(1, 27):
            total = total + arrived[6 * o + s]
        for c in range(3):
            forces_ref[0, 0, c, :, s * BLK : (s + 1) * BLK] = (
                total[c : c + 1] + own_parts[c][s : s + 1]
            )

    pltpu.make_async_copy(
        held.at[pl.ds(0, incoming)], held.at[pl.ds(0, incoming)], send_sem
    ).wait()
    pltpu.make_async_copy(
        partial.at[pl.ds(0, 6 * 26)], partial.at[pl.ds(0, 6 * 26)], back_send_sem
    ).wait()


def on_device(sizes, positions, *arrays):
    *arrays, w_in, w_hidden, w_env, w_latent, w_out = arrays
    vmem = pltpu.VMEM
    forces, energy = pl.pallas_call(
        functools.partial(kernel, sizes),
        out_shape=(
            jax.ShapeDtypeStruct((1, 1, 3, 1, 6 * BLK), F32),
            jax.ShapeDtypeStruct((1, 1, 1), F32),
        ),
        in_specs=[pl.BlockSpec(memory_space=pltpu.HBM)] * 11,
        out_specs=(pl.BlockSpec(memory_space=vmem),) * 2,
        scratch_shapes=[
            vmem((3, 1, NB * BLK), F32),
            vmem((1, NB * BLK), jnp.int32),
            pltpu.SMEM((1, NB), jnp.int32),
            vmem((1, PAIRS), jnp.int32),
            vmem((1, PAIRS), jnp.int32),
            pltpu.SMEM((1, 1), jnp.int32),
            vmem((NBASIS + 2 * NSPEC, CH), BF16),
            vmem((CH, CH), BF16),
            vmem((2, MULT, CH), BF16),
            vmem((2, CH + MULT, CH), BF16),
            vmem((2, CH // 2), BF16),
            vmem((16, CH), BF16),
            vmem((CH, BLK), BF16),
            vmem((CH, CH), BF16),
            vmem((2, CH, CH + BLK), BF16),
            vmem((2, CH, CH + BLK), BF16),
            vmem((6, 4, BLK), F32),
            vmem((ROWS, 4, BLK), F32),
            vmem((2 * BLK, PAIRS), BF16),
            vmem((2 * BLK, PAIRS), BF16),
            vmem((PAIRS, PAIRS), F32),
            vmem((CH, PAIRS), F32),
            vmem((CH, PAIRS), F32),
            vmem((CH, PAIRS), F32),
            vmem((CH, PAIRS), F32),
            vmem((CH, PAIRS), F32),
            vmem((CH, PAIRS), BF16),
            vmem((2, CH, PAIRS), F32),
            vmem((2, MULT, PAIRS), F32),
            vmem((2, MULT, PAIRS), F32),
            vmem((4 * MULT, PAIRS), F32),
            vmem((4 * MULT, PAIRS), BF16),
            vmem((6 * 27, 4, BLK), F32),
            vmem((6 * 27, 4, BLK), F32),
            pltpu.SemaphoreType.DMA((11,)),
            pltpu.SemaphoreType.DMA,
            pltpu.SemaphoreType.DMA,
            pltpu.SemaphoreType.DMA,
            pltpu.SemaphoreType.DMA,
        ],
        compiler_params=pltpu.CompilerParams(
            collective_id=0, has_side_effects=True, vmem_limit_bytes=63 * 1024 * 1024
        ),
        cost_estimate=pl.CostEstimate(flops=10**9, bytes_accessed=10**6, transcendentals=10**6),
    )(
        positions.transpose(0, 1, 3, 2, 4),
        *arrays,
        w_in.T,
        w_hidden,
        w_env,
        w_latent.transpose(0, 2, 1),
        w_out.reshape(2, CH // 2),
    )
    return forces.transpose(0, 1, 3, 2, 4), energy


def solution(mesh):
    sizes = tuple(mesh.shape[axis] for axis in ("gx", "gy", "gz"))
    return jax.shard_map(
        functools.partial(on_device, sizes),
        mesh=mesh,
        in_specs=(
            P("gx", "gy", "gz", None, None),
            P("gx", "gy", "gz", None),
            P("gx", "gy", "gz", None),
            P("gx", "gy", "gz", None),
            P("gx", "gy", "gz", None),
            P("gx", "gy", "gz"),
            P(),
            P(),
            P(),
            P(),
            P(),
        ),
        out_specs=(P("gx", "gy", "gz", None, None), P("gx", "gy", "gz")),
        check_vma=False,
    )
```

```python
import functools

import jax
import jax.numpy as jnp
from jax import lax
from jax.experimental import pallas as pl
from jax.experimental.pallas import tpu as pltpu
from jax.sharding import PartitionSpec as P

MESH = pl.DeviceIdType.MESH

CH = 256
MULT = 64
NBASIS = 8
NSPEC = 3
BLK = 128
NB = 4
PAIRS = 512
CHUNK = 256
CHUNKS = PAIRS // CHUNK

EDGE = 1.5
CUTOFF = 9.0
SOFT2 = 0.25

GROUP = 18
FIRST = {-2: 0, -1: 1, 0: 6, 1: 12, 2: 17}
SENT = {-2: (5, 1), -1: (1, 5), 0: (0, 6), 1: (0, 5), 2: (0, 1)}
ROWS = 9 * GROUP
PADDED = 176
OWN = 4 * GROUP + FIRST[0]

F32 = jnp.float32
BF16 = jnp.bfloat16


def dot(a, b):
    return lax.dot_general(a, b, (((1,), (0,)), ((), ())), preferred_element_type=F32)


def dot_tn(a, b):
    return lax.dot_general(a, b, (((0,), (0,)), ((), ())), preferred_element_type=F32)


def dot_nt(a, b):
    return lax.dot_general(a, b, (((1,), (1,)), ((), ())), preferred_element_type=F32)


def halves(x):
    high = x.astype(BF16)
    return high, (x - high.astype(F32)).astype(BF16)


def rows_of(shape):
    return lax.broadcasted_iota(jnp.int32, shape, 0)


def series(u, terms):
    total = jnp.full_like(u, terms[-1])
    for term in terms[-2::-1]:
        total = total * u + term
    return total


def sin_cos_half_turns(t):
    k = jnp.floor(t + 0.5)
    f = (t - k) * 3.14159265358979
    sign = 1.0 - 2.0 * (k - 2.0 * jnp.floor(0.5 * k))
    u = f * f
    sine = f * series(u, [1.0, -1 / 6, 1 / 120, -1 / 5040, 1 / 362880, -1 / 39916800, 1 / 6227020800])
    cosine = series(
        u, [1.0, -1 / 2, 1 / 24, -1 / 720, 1 / 40320, -1 / 3628800, 1 / 479001600, -1 / 87178291200]
    )
    return sign * sine, sign * cosine


def silu_parts(x):
    gate = 0.5 + 0.5 * jnp.tanh(0.5 * x)
    value = x * gate
    return value, gate + value * (1.0 - gate)


def kernel(
    sizes,
    pos_hbm, kind_hbm, plan_hbm, centre_hbm, neighbour_hbm, blocks_hbm,
    w_in_hbm, w_hidden_hbm, w_env_hbm, w_latent_hbm, w_out_hbm,
    forces_ref, energy_ref,
    pos, kind, plan, centre, neighbour, blocks,
    w_in_raw, w_hidden, w_env, w_latent_t, w_out,
    w_in_t, w_in, w_hidden_t, w_back, w_latent,
    mine, held, lane_neighbour, lane_centre, same,
    d1, d2, h2, latent, grad, inners, dz, env_w, env_a, stacked_a, stacked_b, left,
    partial, arrived,
    in_sems, send_sem, recv_sem, back_send_sem, back_recv_sem,
):
    place = [lax.axis_index(axis) for axis in ("gx", "gy", "gz")]

    def device(steps):
        return tuple(
            lax.rem(at + (step + size), size) if step else at
            for at, step, size in zip(place, steps, sizes)
        )

    far = [(a, b, c) for b in (-1, 0, 1) for c in (-1, 0, 1) for a in (-2, -1, 0, 1, 2)]
    far = [o for o in far if o != (0, 0, 0)]
    far.sort(key=lambda o: -(abs(o[0]) + abs(o[1]) + abs(o[2])))
    near = [o for o in far if abs(o[0]) < 2]

    pairs_in = [
        (pos_hbm.at[0, 0], pos),
        (kind_hbm.at[0, 0], kind),
        (plan_hbm.at[0, 0], plan),
        (centre_hbm.at[0, 0], centre),
        (neighbour_hbm.at[0, 0], neighbour),
        (w_in_hbm, w_in_raw),
        (w_hidden_hbm, w_hidden),
        (w_env_hbm, w_env),
        (w_latent_hbm, w_latent_t),
        (w_out_hbm, w_out),
    ]
    loads = [
        pltpu.make_async_copy(source, target, in_sems.at[i])
        for i, (source, target) in enumerate(pairs_in)
    ]
    for load in loads:
        load.start()

    barrier = pltpu.get_barrier_semaphore()
    for offset in far:
        pl.semaphore_signal(barrier, inc=1, device_id=device(offset), device_id_type=MESH)

    for load in loads[:3]:
        load.wait()
    kind_rows = kind[...].astype(F32) + 1.0
    for b in range(NB):
        lanes_of = slice(b * BLK, (b + 1) * BLK)
        for c in range(3):
            mine[1 + b, c : c + 1] = pos[c, :, lanes_of]
        mine[1 + b, 3:4] = kind_rows[:, lanes_of]
    first_row = (rows_of((4, BLK)) == 0).astype(F32)
    for slot, move, shift in ((0, 1, -EDGE), (5, 2, EDGE)):
        packed = jnp.zeros((4, BLK), F32)
        for b in range(NB):
            chosen = jnp.where(plan[0, b] == move, 1.0, 0.0).astype(F32)
            packed = packed + chosen * (mine[1 + b] + shift * first_row)
        mine[slot] = packed
    held[OWN : OWN + 6] = mine[...]

    pl.semaphore_wait(barrier, len(far))
    for offset in far:
        a, b, c = offset
        start, count = SENT[a]
        where = (3 * (1 - b) + (1 - c)) * GROUP + FIRST[-a]
        pltpu.make_async_remote_copy(
            src_ref=mine.at[pl.ds(start, count)],
            dst_ref=held.at[pl.ds(where, count)],
            send_sem=send_sem,
            recv_sem=recv_sem,
            device_id=device(offset),
            device_id_type=MESH,
        ).start()

    for load in loads[3:]:
        load.wait()
    centre_row = centre[...]
    neighbour_row = neighbour[...]
    live = jnp.where(
        lax.broadcasted_iota(jnp.int32, (1, PAIRS), 1) < blocks_hbm[0, 0, 0] * BLK, 1.0, 0.0
    ).astype(F32)
    centre_block = centre_row >> 7
    centre_lane = centre_row & 127
    block = neighbour_row >> 7
    neighbour_lane = neighbour_row & 127
    box = (block * 10923) >> 16
    k = block - 6 * box
    box_x = (box * 7282) >> 16
    box_yz = box - 9 * box_x
    box_y = (box_yz * 21846) >> 16
    box_z = box_yz - 3 * box_y

    def held_row(x, yz, k):
        up = jnp.where(x == 2, 6, x)
        down = jnp.where(x == 0, 11, 15 + x)
        return yz * GROUP + jnp.where(k == 0, up, jnp.where(k == 5, down, 1 + 5 * x + k))

    neighbour_held = held_row(box_x, box_yz, k)
    centre_held = held_row(jnp.ones_like(centre_block), jnp.zeros_like(centre_block), centre_block)
    lanes = rows_of((BLK, PAIRS))
    hot = jnp.where(lanes == neighbour_lane, 1.0, 0.0).astype(BF16)
    lane_neighbour[:BLK] = hot
    lane_neighbour[BLK:] = hot
    hot = jnp.where(lanes == centre_lane, 1.0, 0.0).astype(BF16)
    lane_centre[:BLK] = hot
    lane_centre[BLK:] = hot
    centre_column = jnp.transpose(
        jnp.broadcast_to(centre_row.astype(F32), (8, PAIRS)), (1, 0)
    )[:, 0:1]
    same[...] = jnp.where(centre_column == centre_row.astype(F32), 1.0, 0.0).astype(F32)

    w_hidden_t[...] = jnp.transpose(w_hidden[...].astype(F32), (1, 0)).astype(BF16)
    for l in range(2):
        padding = jnp.zeros((BLK - MULT, CH), F32)
        rows = jnp.concatenate([w_env[l].astype(F32), padding], axis=0)
        w_back[l, :, :CH] = w_latent_t[l, :CH]
        w_back[l, :, CH:] = jnp.transpose(rows, (1, 0)).astype(BF16)
        rows = jnp.concatenate([w_latent_t[l].astype(F32), padding], axis=0)
        w_latent[l] = jnp.transpose(rows, (1, 0)).astype(BF16)
    fewer = NBASIS + 2 * NSPEC
    rows = jnp.concatenate([w_in_raw[...].astype(F32), jnp.zeros((BLK - fewer, CH), F32)], axis=0)
    w_in_t[...] = rows[:16].astype(BF16)
    w_in[...] = jnp.transpose(rows, (1, 0)).astype(BF16)
    no_rows = jnp.zeros((BLK - MULT, CHUNK), BF16)
    out_row = jnp.concatenate([w_out[0:1], w_out[1:2]], axis=1)
    out_column = jnp.transpose(jnp.broadcast_to(out_row.astype(F32), (8, CH)), (1, 0))[:, 0:1]
    grad[...] = out_column * live

    incoming = ROWS - 6
    pltpu.make_async_copy(
        held.at[pl.ds(0, incoming)], held.at[pl.ds(0, incoming)], recv_sem
    ).wait()

    neighbour_mask = rows_of((ROWS, PAIRS)) == neighbour_held
    centre_mask = rows_of((GROUP, PAIRS)) == centre_held
    near_rows = []
    own_rows = []
    for c in range(4):
        table = held[:, c, :]
        high, low = halves(table)
        both = jnp.concatenate([high, low], axis=1)
        found = dot(both, lane_neighbour[...])
        near_rows.append(jnp.sum(jnp.where(neighbour_mask, found, 0.0), axis=0, keepdims=True))
        table = held[4 * GROUP : 5 * GROUP, c, :]
        high, low = halves(table)
        both = jnp.concatenate([high, low], axis=1)
        found = dot(both, lane_centre[...])
        own_rows.append(jnp.sum(jnp.where(centre_mask, found, 0.0), axis=0, keepdims=True))

    shifts = [EDGE * (v.astype(F32) - 1.0) for v in (box_x, box_y, box_z)]
    gap = [near_rows[c] + shifts[c] - own_rows[c] for c in range(3)]
    square = gap[0] * gap[0] + gap[1] * gap[1] + gap[2] * gap[2]
    inverse = lax.rsqrt(square + SOFT2)
    distance = (square + SOFT2) * inverse
    way = [g * inverse for g in gap]
    scaled = distance * (1.0 / CUTOFF)
    falling = 1.0 - scaled * scaled
    envelope = falling * falling
    orders = (rows_of((NBASIS, PAIRS)) + 1).astype(F32)
    sine, cosine = sin_cos_half_turns(orders * scaled)
    over = sine * inverse
    radial = over * envelope
    r8 = rows_of((8, PAIRS)).astype(F32)
    own_kind = own_rows[3] - 1.0
    near_kind = near_rows[3] - 1.0
    one_hots = jnp.where(
        r8 < NSPEC,
        jnp.where(r8 == own_kind, 1.0, 0.0),
        jnp.where(r8 - NSPEC == near_kind, jnp.where(r8 < 2 * NSPEC, 1.0, 0.0), 0.0),
    )
    features = jnp.concatenate(
        [radial, one_hots, jnp.zeros((BLK - 16, PAIRS), F32)], axis=0
    ).astype(BF16)

    y4 = jnp.concatenate([jnp.ones_like(distance)] + way, axis=0)
    y_high, y_low = halves(y4)
    none = jnp.zeros_like(y_high)
    products = dot_tn(
        jnp.concatenate([y_high, y_high, y_low, none], axis=0).astype(F32),
        jnp.concatenate([y_high, y_low, y_high, none], axis=0).astype(F32),
    )
    g_matrix = (same[...] * products).astype(BF16)

    spans = [slice(j * CHUNK, (j + 1) * CHUNK) for j in range(CHUNKS)]

    before = []
    for s in spans:
        value, slope = silu_parts(dot(w_in[...], features[:, s]))
        d1[:, s] = slope
        value, slope = silu_parts(dot(w_hidden[...], value.astype(BF16)))
        d2[:, s] = slope
        h2[:, s] = value
        latent[:, s] = value * envelope[:, s]
    for l in range(2):
        for j, s in enumerate(spans):
            half = latent[:, s].astype(BF16)
            env_w[l, :, s] = dot(w_env[l], half) * live[:, s]
            dz[l, :, s] = dot(w_latent[l, :, :CH], half)
        weights_half = env_w[l].astype(BF16)
        for j, s in enumerate(spans):
            gathered = dot(weights_half, g_matrix[:, s])
            env_a[l, :, s] = gathered
            invariant = (0.5 * env_w[l, :, s] * gathered).astype(BF16)
            value, slope = silu_parts(dz[l, :, s] + dot(w_latent[l, :, CH:], jnp.concatenate([invariant, no_rows], axis=0)))
            dz[l, :, s] = slope
            latent[:, s] = latent[:, s] + value
    for l in range(2):
        stacked_a[l * MULT : (l + 1) * MULT, :] = env_w[l]
        stacked_b[(2 + l) * MULT : (3 + l) * MULT, :] = env_w[l].astype(BF16)
    left[:, : 2 * MULT] = jnp.transpose(stacked_a[: 2 * MULT], (1, 0)).astype(BF16)

    for l in (1, 0):
        for s in spans:
            inner = (grad[:, s] * dz[l, :, s]).astype(BF16)
            inners[:, s] = inner
            d_invariant = 0.5 * dot(w_latent_t[l, CH:], inner)
            stacked_a[(2 + l) * MULT : (3 + l) * MULT, s] = d_invariant * env_w[l, :, s]
            env_a[l, :, s] = d_invariant * env_a[l, :, s]
        d_gathered = stacked_a[(2 + l) * MULT : (3 + l) * MULT, :].astype(BF16)
        stacked_b[l * MULT : (l + 1) * MULT, :] = d_gathered
        if l == 0:
            left[:, 2 * MULT :] = jnp.transpose(stacked_a[2 * MULT :], (1, 0)).astype(BF16)
            d_products = (same[...] * dot(left[...], stacked_b[...])).astype(BF16)
            d_y = dot(y_high, d_products)
            d_way = [d_y[1 + c : 2 + c] for c in range(3)]
        for s in spans:
            d_weights = (env_a[l, :, s] + dot(d_gathered, g_matrix[:, s])) * live[:, s]
            both = jnp.concatenate([inners[:, s], d_weights.astype(BF16), no_rows], axis=0)
            grad[:, s] = grad[:, s] + dot(w_back[l], both)
    d_radial = []
    d_envelope = []
    for s in spans:
        d_latent = grad[:, s]
        d_envelope.append(jnp.sum(d_latent * h2[:, s], axis=0, keepdims=True))
        inner = (d_latent * envelope[:, s] * d2[:, s]).astype(BF16)
        inner = (dot(w_hidden_t[...], inner) * d1[:, s]).astype(BF16)
        d_radial.append(dot(w_in_t[...], inner)[:NBASIS])
    d_radial = jnp.concatenate(d_radial, axis=1)
    d_envelope = jnp.concatenate(d_envelope, axis=1)

    slope_envelope = falling * scaled * (-4.0 / CUTOFF)
    d_envelope = d_envelope + jnp.sum(d_radial * over, axis=0, keepdims=True)
    d_over = d_radial * envelope
    turning = cosine * orders * (3.14159265358979 / CUTOFF) - over
    d_distance = (
        d_envelope * slope_envelope
        + inverse * jnp.sum(d_over * turning, axis=0, keepdims=True)
        - inverse * (d_way[0] * way[0] + d_way[1] * way[1] + d_way[2] * way[2])
    )
    gradient = [d_way[c] * inverse + d_distance * way[c] for c in range(3)]

    block_mask = rows_of((PADDED, PAIRS)) == block
    for c in range(3):
        spread = jnp.where(block_mask, -gradient[c], 0.0).astype(BF16)
        partial[:, c, :] = dot_nt(spread, lane_neighbour[:BLK])[:ROWS]
    for offset in near:
        a, b, c = offset
        at = 9 * (a + 1) + 3 * (b + 1) + (c + 1)
        pltpu.make_async_remote_copy(
            src_ref=partial.at[pl.ds(6 * at, 6)],
            dst_ref=arrived.at[pl.ds(6 * at, 6)],
            send_sem=back_send_sem,
            recv_sem=back_recv_sem,
            device_id=device(offset),
            device_id_type=MESH,
        ).start()
    arrived[6 * 13 : 6 * 14] = partial[6 * 13 : 6 * 14]
    own_mask = rows_of((16, PAIRS)) == centre_block
    own_parts = []
    for c in range(3):
        spread = jnp.where(own_mask, gradient[c], 0.0).astype(BF16)
        own_parts.append(dot_nt(spread, lane_centre[:BLK]))
    energy = jnp.zeros((1, 1), F32)
    for s in spans:
        values = dot(out_row, latent[:, s].astype(BF16))
        energy = energy + jnp.sum(values * live[:, s], axis=1, keepdims=True)
    energy_ref[...] = jnp.broadcast_to(energy, (1, BLK))

    pltpu.make_async_copy(
        arrived.at[pl.ds(0, 6 * 26)], arrived.at[pl.ds(0, 6 * 26)], back_recv_sem
    ).wait()
    for s in range(6):
        total = arrived[s]
        for o in range(1, 27):
            total = total + arrived[6 * o + s]
        for c in range(3):
            forces_ref[0, 0, c, :, s * BLK : (s + 1) * BLK] = (
                total[c : c + 1] + own_parts[c][s : s + 1]
            )

    pltpu.make_async_copy(
        held.at[pl.ds(0, incoming)], held.at[pl.ds(0, incoming)], send_sem
    ).wait()
    pltpu.make_async_copy(
        partial.at[pl.ds(0, 6 * 26)], partial.at[pl.ds(0, 6 * 26)], back_send_sem
    ).wait()


def hand_over(forces_in, energy_in, forces_out, energy_out):
    forces_out[...] = forces_in[...]
    energy_out[0] = energy_in[0:1, 0:1]


def on_device(sizes, positions, *arrays):
    *arrays, w_in, w_hidden, w_env, w_latent, w_out = arrays
    vmem = pltpu.VMEM
    forces, energy = pl.pallas_call(
        functools.partial(kernel, sizes),
        out_shape=(
            jax.ShapeDtypeStruct((1, 1, 3, 1, 6 * BLK), F32),
            jax.ShapeDtypeStruct((1, BLK), F32),
        ),
        in_specs=[pl.BlockSpec(memory_space=pltpu.HBM)] * 5
        + [pl.BlockSpec(memory_space=pltpu.SMEM)]
        + [pl.BlockSpec(memory_space=pltpu.HBM)] * 5,
        out_specs=(pl.BlockSpec(memory_space=vmem),) * 2,
        scratch_shapes=[
            vmem((3, 1, NB * BLK), F32),
            vmem((1, NB * BLK), jnp.int32),
            pltpu.SMEM((1, NB), jnp.int32),
            vmem((1, PAIRS), jnp.int32),
            vmem((1, PAIRS), jnp.int32),
            pltpu.SMEM((1, 1), jnp.int32),
            vmem((NBASIS + 2 * NSPEC, CH), BF16),
            vmem((CH, CH), BF16),
            vmem((2, MULT, CH), BF16),
            vmem((2, CH + MULT, CH), BF16),
            vmem((2, CH // 2), BF16),
            vmem((16, CH), BF16),
            vmem((CH, BLK), BF16),
            vmem((CH, CH), BF16),
            vmem((2, CH, CH + BLK), BF16),
            vmem((2, CH, CH + BLK), BF16),
            vmem((6, 4, BLK), F32),
            vmem((ROWS, 4, BLK), F32),
            vmem((2 * BLK, PAIRS), BF16),
            vmem((2 * BLK, PAIRS), BF16),
            vmem((PAIRS, PAIRS), F32),
            vmem((CH, PAIRS), F32),
            vmem((CH, PAIRS), F32),
            vmem((CH, PAIRS), F32),
            vmem((CH, PAIRS), F32),
            vmem((CH, PAIRS), F32),
            vmem((CH, PAIRS), BF16),
            vmem((2, CH, PAIRS), F32),
            vmem((2, MULT, PAIRS), F32),
            vmem((2, MULT, PAIRS), F32),
            vmem((4 * MULT, PAIRS), F32),
            vmem((4 * MULT, PAIRS), BF16),
            vmem((PAIRS, 4 * MULT), BF16),
            vmem((6 * 27, 4, BLK), F32),
            vmem((6 * 27, 4, BLK), F32),
            pltpu.SemaphoreType.DMA((11,)),
            pltpu.SemaphoreType.DMA,
            pltpu.SemaphoreType.DMA,
            pltpu.SemaphoreType.DMA,
            pltpu.SemaphoreType.DMA,
        ],
        compiler_params=pltpu.CompilerParams(
            collective_id=0, has_side_effects=True, vmem_limit_bytes=63 * 1024 * 1024
        ),
        cost_estimate=pl.CostEstimate(flops=10**9, bytes_accessed=10**6, transcendentals=10**6),
    )(
        positions.transpose(0, 1, 3, 2, 4),
        *arrays,
        w_in.T,
        w_hidden,
        w_env,
        w_latent.transpose(0, 2, 1),
        w_out.reshape(2, CH // 2),
    )
    forces, energy = pl.pallas_call(
        hand_over,
        out_shape=(
            jax.ShapeDtypeStruct((1, 1, 3, 1, 6 * BLK), F32),
            jax.ShapeDtypeStruct((1, 1, 1), F32),
        ),
        in_specs=(pl.BlockSpec(memory_space=vmem),) * 2,
        out_specs=(pl.BlockSpec(memory_space=vmem),) * 2,
        compiler_params=pltpu.CompilerParams(vmem_limit_bytes=63 * 1024 * 1024),
    )(forces, energy)
    return forces.transpose(0, 1, 3, 2, 4), energy


def solution(mesh):
    sizes = tuple(mesh.shape[axis] for axis in ("gx", "gy", "gz"))
    return jax.shard_map(
        functools.partial(on_device, sizes),
        mesh=mesh,
        in_specs=(
            P("gx", "gy", "gz", None, None),
            P("gx", "gy", "gz", None),
            P("gx", "gy", "gz", None),
            P("gx", "gy", "gz", None),
            P("gx", "gy", "gz", None),
            P("gx", "gy", "gz"),
            P(),
            P(),
            P(),
            P(),
            P(),
        ),
        out_specs=(P("gx", "gy", "gz", None, None), P("gx", "gy", "gz")),
        check_vma=False,
    )
```

```python
import functools

import jax
import jax.numpy as jnp
from jax import lax
from jax.experimental import pallas as pl
from jax.experimental.pallas import tpu as pltpu
from jax.sharding import PartitionSpec as P

MESH = pl.DeviceIdType.MESH

CH = 256
MULT = 64
NBASIS = 8
NSPEC = 3
BLK = 128
NB = 4
PAIRS = 512
CHUNK = 256
CHUNKS = PAIRS // CHUNK

EDGE = 1.5
CUTOFF = 9.0
SOFT2 = 0.25

GROUP = 18
FIRST = {-2: 0, -1: 1, 0: 6, 1: 12, 2: 17}
SENT = {-2: (5, 1), -1: (1, 5), 0: (0, 6), 1: (0, 5), 2: (0, 1)}
ROWS = 9 * GROUP
PADDED = 164
OWN = 4 * GROUP + FIRST[0]

F32 = jnp.float32
BF16 = jnp.bfloat16


def dot(a, b):
    return lax.dot_general(a, b, (((1,), (0,)), ((), ())), preferred_element_type=F32)


def dot_tn(a, b):
    return lax.dot_general(a, b, (((0,), (0,)), ((), ())), preferred_element_type=F32)


def dot_nt(a, b):
    return lax.dot_general(a, b, (((1,), (1,)), ((), ())), preferred_element_type=F32)


def halves(x):
    high = x.astype(BF16)
    return high, (x - high.astype(F32)).astype(BF16)


def rows_of(shape):
    return lax.broadcasted_iota(jnp.int32, shape, 0)


def series(u, terms):
    total = jnp.full_like(u, terms[-1])
    for term in terms[-2::-1]:
        total = total * u + term
    return total


def sin_cos_half_turns(t):
    k = jnp.floor(t + 0.5)
    f = (t - k) * 3.14159265358979
    sign = 1.0 - 2.0 * (k - 2.0 * jnp.floor(0.5 * k))
    u = f * f
    sine = f * series(u, [1.0, -1 / 6, 1 / 120, -1 / 5040, 1 / 362880, -1 / 39916800, 1 / 6227020800])
    cosine = series(
        u, [1.0, -1 / 2, 1 / 24, -1 / 720, 1 / 40320, -1 / 3628800, 1 / 479001600, -1 / 87178291200]
    )
    return sign * sine, sign * cosine


def silu_parts(x):
    gate = 0.5 + 0.5 * jnp.tanh(0.5 * x)
    value = x * gate
    return value, gate + value * (1.0 - gate)


def kernel(
    sizes,
    pos_hbm, kind_hbm, plan_hbm, centre_hbm, neighbour_hbm, blocks_hbm,
    w_in_hbm, w_hidden_hbm, w_env_hbm, w_latent_hbm, w_out_hbm,
    forces_ref, energy_ref,
    pos, kind, plan, centre, neighbour, blocks,
    w_in_raw, w_hidden, w_env, w_latent_t, w_out,
    w_in_t, w_in, w_hidden_t, w_back, w_latent,
    mine, held, lane_neighbour, lane_centre, same,
    d1, d2, h2, latent, grad, inners, dz, env_w, env_a, stacked_a, stacked_b, left,
    partial, arrived,
    in_sems, send_sem, recv_sem, back_send_sem, back_recv_sem,
):
    place = [lax.axis_index(axis) for axis in ("gx", "gy", "gz")]

    def device(steps):
        return tuple(
            lax.rem(at + (step + size), size) if step else at
            for at, step, size in zip(place, steps, sizes)
        )

    far = [(a, b, c) for b in (-1, 0, 1) for c in (-1, 0, 1) for a in (-2, -1, 0, 1, 2)]
    far = [o for o in far if o != (0, 0, 0)]
    far.sort(key=lambda o: -(abs(o[0]) + abs(o[1]) + abs(o[2])))
    near = [o for o in far if abs(o[0]) < 2]

    pairs_in = [
        (pos_hbm.at[0, 0], pos),
        (kind_hbm.at[0, 0], kind),
        (plan_hbm.at[0, 0], plan),
        (centre_hbm.at[0, 0], centre),
        (neighbour_hbm.at[0, 0], neighbour),
        (w_in_hbm, w_in_raw),
        (w_hidden_hbm, w_hidden),
        (w_env_hbm, w_env),
        (w_latent_hbm, w_latent_t),
        (w_out_hbm, w_out),
    ]
    loads = [
        pltpu.make_async_copy(source, target, in_sems.at[i])
        for i, (source, target) in enumerate(pairs_in)
    ]
    for load in loads:
        load.start()

    barrier = pltpu.get_barrier_semaphore()
    for offset in far:
        pl.semaphore_signal(barrier, inc=1, device_id=device(offset), device_id_type=MESH)

    for load in loads[:3]:
        load.wait()
    kind_rows = kind[...].astype(F32) + 1.0
    for b in range(NB):
        lanes_of = slice(b * BLK, (b + 1) * BLK)
        for c in range(3):
            mine[1 + b, c : c + 1] = pos[c, :, lanes_of]
        mine[1 + b, 3:4] = kind_rows[:, lanes_of]
    first_row = (rows_of((4, BLK)) == 0).astype(F32)
    for slot, move, shift in ((0, 1, -EDGE), (5, 2, EDGE)):
        packed = jnp.zeros((4, BLK), F32)
        for b in range(NB):
            chosen = jnp.where(plan[0, b] == move, 1.0, 0.0).astype(F32)
            packed = packed + chosen * (mine[1 + b] + shift * first_row)
        mine[slot] = packed
    held[OWN : OWN + 6] = mine[...]
    held[ROWS:] = jnp.zeros((PADDED - ROWS, 4, BLK), F32)

    pl.semaphore_wait(barrier, len(far))
    for offset in far:
        a, b, c = offset
        start, count = SENT[a]
        where = (3 * (1 - b) + (1 - c)) * GROUP + FIRST[-a]
        pltpu.make_async_remote_copy(
            src_ref=mine.at[pl.ds(start, count)],
            dst_ref=held.at[pl.ds(where, count)],
            send_sem=send_sem,
            recv_sem=recv_sem,
            device_id=device(offset),
            device_id_type=MESH,
        ).start()

    for load in loads[3:]:
        load.wait()
    centre_row = centre[...]
    neighbour_row = neighbour[...]
    live = jnp.where(
        lax.broadcasted_iota(jnp.int32, (1, PAIRS), 1) < blocks_hbm[0, 0, 0] * BLK, 1.0, 0.0
    ).astype(F32)
    centre_block = centre_row >> 7
    centre_lane = centre_row & 127
    block = neighbour_row >> 7
    neighbour_lane = neighbour_row & 127
    box = (block * 10923) >> 16
    k = block - 6 * box
    box_x = (box * 7282) >> 16
    box_yz = box - 9 * box_x
    box_y = (box_yz * 21846) >> 16
    box_z = box_yz - 3 * box_y

    def held_row(x, yz, k):
        up = jnp.where(x == 2, 6, x)
        down = jnp.where(x == 0, 11, 15 + x)
        return yz * GROUP + jnp.where(k == 0, up, jnp.where(k == 5, down, 1 + 5 * x + k))

    neighbour_held = held_row(box_x, box_yz, k)
    centre_held = held_row(jnp.ones_like(centre_block), jnp.zeros_like(centre_block), centre_block)
    lanes = rows_of((BLK, PAIRS))
    hot = jnp.where(lanes == neighbour_lane, 1.0, 0.0).astype(BF16)
    lane_neighbour[:BLK] = hot
    lane_neighbour[BLK:] = hot
    hot = jnp.where(lanes == centre_lane, 1.0, 0.0).astype(BF16)
    lane_centre[:BLK] = hot
    lane_centre[BLK:] = hot
    centre_column = jnp.transpose(
        jnp.broadcast_to(centre_row.astype(F32), (8, PAIRS)), (1, 0)
    )[:, 0:1]
    same[...] = jnp.where(centre_column == centre_row.astype(F32), 1.0, 0.0).astype(F32)

    w_hidden_t[...] = jnp.transpose(w_hidden[...].astype(F32), (1, 0)).astype(BF16)
    for l in range(2):
        padding = jnp.zeros((BLK - MULT, CH), F32)
        rows = jnp.concatenate([w_env[l].astype(F32), padding], axis=0)
        w_back[l, :, :CH] = w_latent_t[l, :CH]
        w_back[l, :, CH:] = jnp.transpose(rows, (1, 0)).astype(BF16)
        rows = jnp.concatenate([w_latent_t[l].astype(F32), padding], axis=0)
        w_latent[l] = jnp.transpose(rows, (1, 0)).astype(BF16)
    fewer = NBASIS + 2 * NSPEC
    rows = jnp.concatenate([w_in_raw[...].astype(F32), jnp.zeros((BLK - fewer, CH), F32)], axis=0)
    w_in_t[...] = rows[:16].astype(BF16)
    w_in[...] = jnp.transpose(rows, (1, 0)).astype(BF16)
    no_rows = jnp.zeros((BLK - MULT, CHUNK), BF16)
    out_row = jnp.concatenate([w_out[0:1], w_out[1:2]], axis=1)
    out_column = jnp.transpose(jnp.broadcast_to(out_row.astype(F32), (8, CH)), (1, 0))[:, 0:1]
    grad[...] = out_column * live

    incoming = ROWS - 6
    pltpu.make_async_copy(
        held.at[pl.ds(0, incoming)], held.at[pl.ds(0, incoming)], recv_sem
    ).wait()

    def found_at(table, hot, block_index):
        count = table.shape[0] * 4
        high, low = halves(table.reshape(count, BLK))
        found = dot(jnp.concatenate([high, low], axis=1), hot)
        found = jnp.where(rows_of((count, PAIRS)) >> 2 == block_index, found, 0.0)
        found = jnp.sum(found.reshape(count // 8, 8, PAIRS), axis=0)
        found = found[0:4] + found[4:8]
        return [found[c : c + 1] for c in range(4)]

    near_rows = found_at(held[...], lane_neighbour[...], neighbour_held)
    own_rows = found_at(held[4 * GROUP : 4 * GROUP + 20], lane_centre[...], centre_held)

    shifts = [EDGE * (v.astype(F32) - 1.0) for v in (box_x, box_y, box_z)]
    gap = [near_rows[c] + shifts[c] - own_rows[c] for c in range(3)]
    square = gap[0] * gap[0] + gap[1] * gap[1] + gap[2] * gap[2]
    inverse = lax.rsqrt(square + SOFT2)
    distance = (square + SOFT2) * inverse
    way = [g * inverse for g in gap]
    scaled = distance * (1.0 / CUTOFF)
    falling = 1.0 - scaled * scaled
    envelope = falling * falling
    orders = (rows_of((NBASIS, PAIRS)) + 1).astype(F32)
    sine, cosine = sin_cos_half_turns(orders * scaled)
    over = sine * inverse
    radial = over * envelope
    r8 = rows_of((8, PAIRS)).astype(F32)
    own_kind = own_rows[3] - 1.0
    near_kind = near_rows[3] - 1.0
    one_hots = jnp.where(
        r8 < NSPEC,
        jnp.where(r8 == own_kind, 1.0, 0.0),
        jnp.where(r8 - NSPEC == near_kind, jnp.where(r8 < 2 * NSPEC, 1.0, 0.0), 0.0),
    )
    features = jnp.concatenate(
        [radial, one_hots, jnp.zeros((BLK - 16, PAIRS), F32)], axis=0
    ).astype(BF16)

    y4 = jnp.concatenate([jnp.ones_like(distance)] + way, axis=0)
    y_high, y_low = halves(y4)
    none = jnp.zeros_like(y_high)
    products = dot_tn(
        jnp.concatenate([y_high, y_high, y_low, none], axis=0).astype(F32),
        jnp.concatenate([y_high, y_low, y_high, none], axis=0).astype(F32),
    )
    g_matrix = (same[...] * products).astype(BF16)

    spans = [slice(j * CHUNK, (j + 1) * CHUNK) for j in range(CHUNKS)]

    before = []
    for s in spans:
        value, slope = silu_parts(dot(w_in[...], features[:, s]))
        d1[:, s] = slope
        value, slope = silu_parts(dot(w_hidden[...], value.astype(BF16)))
        d2[:, s] = slope
        h2[:, s] = value
        latent[:, s] = value * envelope[:, s]
    for l in range(2):
        for j, s in enumerate(spans):
            half = latent[:, s].astype(BF16)
            env_w[l, :, s] = dot(w_env[l], half) * live[:, s]
            dz[l, :, s] = dot(w_latent[l, :, :CH], half)
        weights_half = env_w[l].astype(BF16)
        for j, s in enumerate(spans):
            gathered = dot(weights_half, g_matrix[:, s])
            env_a[l, :, s] = gathered
            invariant = (0.5 * env_w[l, :, s] * gathered).astype(BF16)
            value, slope = silu_parts(dz[l, :, s] + dot(w_latent[l, :, CH:], jnp.concatenate([invariant, no_rows], axis=0)))
            dz[l, :, s] = slope
            latent[:, s] = latent[:, s] + value
    for l in range(2):
        stacked_a[l * MULT : (l + 1) * MULT, :] = env_w[l]
        stacked_b[(2 + l) * MULT : (3 + l) * MULT, :] = env_w[l].astype(BF16)
    left[:, : 2 * MULT] = jnp.transpose(stacked_a[: 2 * MULT], (1, 0)).astype(BF16)

    for l in (1, 0):
        for s in spans:
            inner = (grad[:, s] * dz[l, :, s]).astype(BF16)
            inners[:, s] = inner
            d_invariant = 0.5 * dot(w_latent_t[l, CH:], inner)
            stacked_a[(2 + l) * MULT : (3 + l) * MULT, s] = d_invariant * env_w[l, :, s]
            env_a[l, :, s] = d_invariant * env_a[l, :, s]
        d_gathered = stacked_a[(2 + l) * MULT : (3 + l) * MULT, :].astype(BF16)
        stacked_b[l * MULT : (l + 1) * MULT, :] = d_gathered
        if l == 0:
            left[:, 2 * MULT :] = jnp.transpose(stacked_a[2 * MULT :], (1, 0)).astype(BF16)
            d_products = (same[...] * dot(left[...], stacked_b[...])).astype(BF16)
            d_y = dot(y_high, d_products)
            d_way = [d_y[1 + c : 2 + c] for c in range(3)]
        for s in spans:
            d_weights = (env_a[l, :, s] + dot(d_gathered, g_matrix[:, s])) * live[:, s]
            both = jnp.concatenate([inners[:, s], d_weights.astype(BF16), no_rows], axis=0)
            grad[:, s] = grad[:, s] + dot(w_back[l], both)
    d_radial = []
    d_envelope = []
    for s in spans:
        d_latent = grad[:, s]
        d_envelope.append(jnp.sum(d_latent * h2[:, s], axis=0, keepdims=True))
        inner = (d_latent * envelope[:, s] * d2[:, s]).astype(BF16)
        inner = (dot(w_hidden_t[...], inner) * d1[:, s]).astype(BF16)
        d_radial.append(dot(w_in_t[...], inner)[:NBASIS])
    d_radial = jnp.concatenate(d_radial, axis=1)
    d_envelope = jnp.concatenate(d_envelope, axis=1)

    slope_envelope = falling * scaled * (-4.0 / CUTOFF)
    d_envelope = d_envelope + jnp.sum(d_radial * over, axis=0, keepdims=True)
    d_over = d_radial * envelope
    turning = cosine * orders * (3.14159265358979 / CUTOFF) - over
    d_distance = (
        d_envelope * slope_envelope
        + inverse * jnp.sum(d_over * turning, axis=0, keepdims=True)
        - inverse * (d_way[0] * way[0] + d_way[1] * way[1] + d_way[2] * way[2])
    )
    gradient = [d_way[c] * inverse + d_distance * way[c] for c in range(3)]

    def scattered(count, values, hot, block_index):
        pattern = jnp.concatenate(values + [jnp.zeros((1, PAIRS), F32)], axis=0)
        pattern = jnp.concatenate([pattern, pattern], axis=0)
        pattern = jnp.broadcast_to(pattern[None], (count // 2, 8, PAIRS)).reshape(4 * count, PAIRS)
        spread = jnp.where(rows_of((4 * count, PAIRS)) >> 2 == block_index, pattern, 0.0)
        return dot_nt(spread.astype(BF16), hot).reshape(count, 4, BLK)

    partial[...] = scattered(PADDED, [-g for g in gradient], lane_neighbour[:BLK], block)
    for offset in near:
        a, b, c = offset
        at = 9 * (a + 1) + 3 * (b + 1) + (c + 1)
        pltpu.make_async_remote_copy(
            src_ref=partial.at[pl.ds(6 * at, 6)],
            dst_ref=arrived.at[pl.ds(6 * at, 6)],
            send_sem=back_send_sem,
            recv_sem=back_recv_sem,
            device_id=device(offset),
            device_id_type=MESH,
        ).start()
    arrived[6 * 13 : 6 * 14] = partial[6 * 13 : 6 * 14]
    own_part = scattered(8, gradient, lane_centre[:BLK], centre_block)
    energy = jnp.zeros((1, 1), F32)
    for s in spans:
        values = dot(out_row, latent[:, s].astype(BF16))
        energy = energy + jnp.sum(values * live[:, s], axis=1, keepdims=True)
    energy_ref[...] = jnp.broadcast_to(energy, (1, BLK))

    pltpu.make_async_copy(
        arrived.at[pl.ds(0, 6 * 26)], arrived.at[pl.ds(0, 6 * 26)], back_recv_sem
    ).wait()
    for s in range(6):
        total = own_part[s]
        for o in range(27):
            total = total + arrived[6 * o + s]
        for c in range(3):
            forces_ref[0, 0, c, :, s * BLK : (s + 1) * BLK] = total[c : c + 1]

    pltpu.make_async_copy(
        held.at[pl.ds(0, incoming)], held.at[pl.ds(0, incoming)], send_sem
    ).wait()
    pltpu.make_async_copy(
        partial.at[pl.ds(0, 6 * 26)], partial.at[pl.ds(0, 6 * 26)], back_send_sem
    ).wait()


def hand_over(forces_in, energy_in, forces_out, energy_out):
    forces_out[...] = forces_in[...]
    energy_out[0] = energy_in[0:1, 0:1]


def on_device(sizes, positions, *arrays):
    *arrays, w_in, w_hidden, w_env, w_latent, w_out = arrays
    vmem = pltpu.VMEM
    forces, energy = pl.pallas_call(
        functools.partial(kernel, sizes),
        out_shape=(
            jax.ShapeDtypeStruct((1, 1, 3, 1, 6 * BLK), F32),
            jax.ShapeDtypeStruct((1, BLK), F32),
        ),
        in_specs=[pl.BlockSpec(memory_space=pltpu.HBM)] * 5
        + [pl.BlockSpec(memory_space=pltpu.SMEM)]
        + [pl.BlockSpec(memory_space=pltpu.HBM)] * 5,
        out_specs=(pl.BlockSpec(memory_space=vmem),) * 2,
        scratch_shapes=[
            vmem((3, 1, NB * BLK), F32),
            vmem((1, NB * BLK), jnp.int32),
            pltpu.SMEM((1, NB), jnp.int32),
            vmem((1, PAIRS), jnp.int32),
            vmem((1, PAIRS), jnp.int32),
            pltpu.SMEM((1, 1), jnp.int32),
            vmem((NBASIS + 2 * NSPEC, CH), BF16),
            vmem((CH, CH), BF16),
            vmem((2, MULT, CH), BF16),
            vmem((2, CH + MULT, CH), BF16),
            vmem((2, CH // 2), BF16),
            vmem((16, CH), BF16),
            vmem((CH, BLK), BF16),
            vmem((CH, CH), BF16),
            vmem((2, CH, CH + BLK), BF16),
            vmem((2, CH, CH + BLK), BF16),
            vmem((6, 4, BLK), F32),
            vmem((PADDED, 4, BLK), F32),
            vmem((2 * BLK, PAIRS), BF16),
            vmem((2 * BLK, PAIRS), BF16),
            vmem((PAIRS, PAIRS), F32),
            vmem((CH, PAIRS), F32),
            vmem((CH, PAIRS), F32),
            vmem((CH, PAIRS), F32),
            vmem((CH, PAIRS), F32),
            vmem((CH, PAIRS), F32),
            vmem((CH, PAIRS), BF16),
            vmem((2, CH, PAIRS), F32),
            vmem((2, MULT, PAIRS), F32),
            vmem((2, MULT, PAIRS), F32),
            vmem((4 * MULT, PAIRS), F32),
            vmem((4 * MULT, PAIRS), BF16),
            vmem((PAIRS, 4 * MULT), BF16),
            vmem((PADDED, 4, BLK), F32),
            vmem((6 * 27, 4, BLK), F32),
            pltpu.SemaphoreType.DMA((11,)),
            pltpu.SemaphoreType.DMA,
            pltpu.SemaphoreType.DMA,
            pltpu.SemaphoreType.DMA,
            pltpu.SemaphoreType.DMA,
        ],
        compiler_params=pltpu.CompilerParams(
            collective_id=0, has_side_effects=True, vmem_limit_bytes=63 * 1024 * 1024
        ),
        cost_estimate=pl.CostEstimate(flops=10**9, bytes_accessed=10**6, transcendentals=10**6),
    )(
        positions.transpose(0, 1, 3, 2, 4),
        *arrays,
        w_in.T,
        w_hidden,
        w_env,
        w_latent.transpose(0, 2, 1),
        w_out.reshape(2, CH // 2),
    )
    forces, energy = pl.pallas_call(
        hand_over,
        out_shape=(
            jax.ShapeDtypeStruct((1, 1, 3, 1, 6 * BLK), F32),
            jax.ShapeDtypeStruct((1, 1, 1), F32),
        ),
        in_specs=(pl.BlockSpec(memory_space=vmem),) * 2,
        out_specs=(pl.BlockSpec(memory_space=vmem),) * 2,
        compiler_params=pltpu.CompilerParams(vmem_limit_bytes=63 * 1024 * 1024),
    )(forces, energy)
    return forces.transpose(0, 1, 3, 2, 4), energy


def solution(mesh):
    sizes = tuple(mesh.shape[axis] for axis in ("gx", "gy", "gz"))
    return jax.shard_map(
        functools.partial(on_device, sizes),
        mesh=mesh,
        in_specs=(
            P("gx", "gy", "gz", None, None),
            P("gx", "gy", "gz", None),
            P("gx", "gy", "gz", None),
            P("gx", "gy", "gz", None),
            P("gx", "gy", "gz", None),
            P("gx", "gy", "gz"),
            P(),
            P(),
            P(),
            P(),
            P(),
        ),
        out_specs=(P("gx", "gy", "gz", None, None), P("gx", "gy", "gz")),
        check_vma=False,
    )
```

```python
import functools

import jax
import jax.numpy as jnp
from jax import lax
from jax.experimental import pallas as pl
from jax.experimental.pallas import tpu as pltpu
from jax.sharding import PartitionSpec as P

MESH = pl.DeviceIdType.MESH

CH = 256
MULT = 64
NBASIS = 8
NSPEC = 3
BLK = 128
NB = 4
PAIRS = 512
CHUNK = 256
CHUNKS = PAIRS // CHUNK

EDGE = 1.5
CUTOFF = 9.0
SOFT2 = 0.25

GROUP = 18
FIRST = {-2: 0, -1: 1, 0: 6, 1: 12, 2: 17}
SENT = {-2: (5, 1), -1: (1, 5), 0: (0, 6), 1: (0, 5), 2: (0, 1)}
ROWS = 9 * GROUP
PADDED = 164
OWN = 4 * GROUP + FIRST[0]

F32 = jnp.float32
BF16 = jnp.bfloat16


def dot(a, b):
    return lax.dot_general(a, b, (((1,), (0,)), ((), ())), preferred_element_type=F32)


def dot_tn(a, b):
    return lax.dot_general(a, b, (((0,), (0,)), ((), ())), preferred_element_type=F32)


def dot_nt(a, b):
    return lax.dot_general(a, b, (((1,), (1,)), ((), ())), preferred_element_type=F32)


def halves(x):
    high = x.astype(BF16)
    return high, (x - high.astype(F32)).astype(BF16)


def rows_of(shape):
    return lax.broadcasted_iota(jnp.int32, shape, 0)


def series(u, terms):
    total = jnp.full_like(u, terms[-1])
    for term in terms[-2::-1]:
        total = total * u + term
    return total


def sin_cos_half_turns(t):
    k = jnp.floor(t + 0.5)
    f = (t - k) * 3.14159265358979
    sign = 1.0 - 2.0 * (k - 2.0 * jnp.floor(0.5 * k))
    u = f * f
    sine = f * series(u, [1.0, -1 / 6, 1 / 120, -1 / 5040, 1 / 362880, -1 / 39916800, 1 / 6227020800])
    cosine = series(
        u, [1.0, -1 / 2, 1 / 24, -1 / 720, 1 / 40320, -1 / 3628800, 1 / 479001600, -1 / 87178291200]
    )
    return sign * sine, sign * cosine


def silu_parts(x):
    gate = 0.5 + 0.5 * jnp.tanh(0.5 * x)
    value = x * gate
    return value, gate + value * (1.0 - gate)


def kernel(
    sizes,
    pos_hbm, kind_hbm, plan_hbm, centre_hbm, neighbour_hbm, blocks_hbm,
    w_in_hbm, w_hidden_hbm, w_env_hbm, w_latent_hbm, w_out_hbm,
    results,
    pos, kind, plan, centre, neighbour, blocks,
    w_in_raw, w_hidden, w_env, w_latent_t, w_out,
    w_in_t, w_in, w_hidden_t, w_back, w_latent,
    mine, held, lane_neighbour, lane_centre, same,
    d1, d2, h2, latent, grad, inners, dz, env_w, env_a, stacked_a, stacked_b, left,
    partial, arrived,
    in_sems, send_sem, recv_sem, back_send_sem, back_recv_sem,
):
    place = [lax.axis_index(axis) for axis in ("gx", "gy", "gz")]

    def device(steps):
        return tuple(
            lax.rem(at + (step + size), size) if step else at
            for at, step, size in zip(place, steps, sizes)
        )

    far = [(a, b, c) for b in (-1, 0, 1) for c in (-1, 0, 1) for a in (-2, -1, 0, 1, 2)]
    far = [o for o in far if o != (0, 0, 0)]
    far.sort(key=lambda o: -(2 * (abs(o[1]) + abs(o[2])) + abs(o[0])))
    far = [x for o in far if o > (0, 0, 0) for x in (o, (-o[0], -o[1], -o[2]))]
    near = [o for o in far if abs(o[0]) < 2]

    pairs_in = [
        (pos_hbm.at[0, 0], pos),
        (kind_hbm.at[0, 0], kind),
        (plan_hbm.at[0, 0], plan),
        (centre_hbm.at[0, 0], centre),
        (neighbour_hbm.at[0, 0], neighbour),
        (w_in_hbm, w_in_raw),
        (w_hidden_hbm, w_hidden),
        (w_env_hbm, w_env),
        (w_latent_hbm, w_latent_t),
        (w_out_hbm, w_out),
    ]
    loads = [
        pltpu.make_async_copy(source, target, in_sems.at[i])
        for i, (source, target) in enumerate(pairs_in)
    ]
    for load in loads:
        load.start()

    barrier = pltpu.get_barrier_semaphore()
    for offset in far:
        pl.semaphore_signal(barrier, inc=1, device_id=device(offset), device_id_type=MESH)

    for load in loads[:3]:
        load.wait()
    kind_rows = kind[...].astype(F32) + 1.0
    for b in range(NB):
        lanes_of = slice(b * BLK, (b + 1) * BLK)
        for c in range(3):
            mine[1 + b, c : c + 1] = pos[c, :, lanes_of]
        mine[1 + b, 3:4] = kind_rows[:, lanes_of]
    first_row = (rows_of((4, BLK)) == 0).astype(F32)
    for slot, move, shift in ((0, 1, -EDGE), (5, 2, EDGE)):
        packed = jnp.zeros((4, BLK), F32)
        for b in range(NB):
            chosen = jnp.where(plan[0, b] == move, 1.0, 0.0).astype(F32)
            packed = packed + chosen * (mine[1 + b] + shift * first_row)
        mine[slot] = packed
    held[OWN : OWN + 6] = mine[...]
    held[ROWS:] = jnp.zeros((PADDED - ROWS, 4, BLK), F32)

    pl.semaphore_wait(barrier, len(far))
    for offset in far:
        a, b, c = offset
        start, count = SENT[a]
        where = (3 * (1 - b) + (1 - c)) * GROUP + FIRST[-a]
        pltpu.make_async_remote_copy(
            src_ref=mine.at[pl.ds(start, count)],
            dst_ref=held.at[pl.ds(where, count)],
            send_sem=send_sem,
            recv_sem=recv_sem,
            device_id=device(offset),
            device_id_type=MESH,
        ).start()

    for load in loads[3:]:
        load.wait()
    centre_row = centre[...]
    neighbour_row = neighbour[...]
    live = jnp.where(
        lax.broadcasted_iota(jnp.int32, (1, PAIRS), 1) < blocks_hbm[0, 0, 0] * BLK, 1.0, 0.0
    ).astype(F32)
    centre_block = centre_row >> 7
    centre_lane = centre_row & 127
    block = neighbour_row >> 7
    neighbour_lane = neighbour_row & 127
    box = (block * 10923) >> 16
    k = block - 6 * box
    box_x = (box * 7282) >> 16
    box_yz = box - 9 * box_x
    box_y = (box_yz * 21846) >> 16
    box_z = box_yz - 3 * box_y

    def held_row(x, yz, k):
        up = jnp.where(x == 2, 6, x)
        down = jnp.where(x == 0, 11, 15 + x)
        return yz * GROUP + jnp.where(k == 0, up, jnp.where(k == 5, down, 1 + 5 * x + k))

    neighbour_held = held_row(box_x, box_yz, k)
    centre_held = held_row(jnp.ones_like(centre_block), jnp.zeros_like(centre_block), centre_block)
    lanes = rows_of((BLK, PAIRS))
    hot = jnp.where(lanes == neighbour_lane, 1.0, 0.0).astype(BF16)
    lane_neighbour[:BLK] = hot
    lane_neighbour[BLK:] = hot
    hot = jnp.where(lanes == centre_lane, 1.0, 0.0).astype(BF16)
    lane_centre[:BLK] = hot
    lane_centre[BLK:] = hot
    centre_column = jnp.transpose(
        jnp.broadcast_to(centre_row.astype(F32), (8, PAIRS)), (1, 0)
    )[:, 0:1]
    same[...] = jnp.where(centre_column == centre_row.astype(F32), 1.0, 0.0).astype(F32)

    w_hidden_t[...] = jnp.transpose(w_hidden[...].astype(F32), (1, 0)).astype(BF16)
    for l in range(2):
        padding = jnp.zeros((BLK - MULT, CH), F32)
        rows = jnp.concatenate([w_env[l].astype(F32), padding], axis=0)
        w_back[l, :, :CH] = w_latent_t[l, :CH]
        w_back[l, :, CH:] = jnp.transpose(rows, (1, 0)).astype(BF16)
        rows = jnp.concatenate([w_latent_t[l].astype(F32), padding], axis=0)
        w_latent[l] = jnp.transpose(rows, (1, 0)).astype(BF16)
    fewer = NBASIS + 2 * NSPEC
    rows = jnp.concatenate([w_in_raw[...].astype(F32), jnp.zeros((BLK - fewer, CH), F32)], axis=0)
    w_in_t[...] = rows[:16].astype(BF16)
    w_in[...] = jnp.transpose(rows, (1, 0)).astype(BF16)
    no_rows = jnp.zeros((BLK - MULT, CHUNK), BF16)
    out_row = jnp.concatenate([w_out[0:1], w_out[1:2]], axis=1)
    out_column = jnp.transpose(jnp.broadcast_to(out_row.astype(F32), (8, CH)), (1, 0))[:, 0:1]
    grad[...] = out_column * live

    incoming = ROWS - 6
    pltpu.make_async_copy(
        held.at[pl.ds(0, incoming)], held.at[pl.ds(0, incoming)], recv_sem
    ).wait()

    def found_at(table, hot, block_index):
        count = table.shape[0] * 4
        high, low = halves(table.reshape(count, BLK))
        found = dot(jnp.concatenate([high, low], axis=1), hot)
        found = jnp.where(rows_of((count, PAIRS)) >> 2 == block_index, found, 0.0)
        found = jnp.sum(found.reshape(count // 8, 8, PAIRS), axis=0)
        found = found[0:4] + found[4:8]
        return [found[c : c + 1] for c in range(4)]

    near_rows = found_at(held[...], lane_neighbour[...], neighbour_held)
    own_rows = found_at(held[4 * GROUP : 4 * GROUP + 20], lane_centre[...], centre_held)

    shifts = [EDGE * (v.astype(F32) - 1.0) for v in (box_x, box_y, box_z)]
    gap = [near_rows[c] + shifts[c] - own_rows[c] for c in range(3)]
    square = gap[0] * gap[0] + gap[1] * gap[1] + gap[2] * gap[2]
    inverse = lax.rsqrt(square + SOFT2)
    distance = (square + SOFT2) * inverse
    way = [g * inverse for g in gap]
    scaled = distance * (1.0 / CUTOFF)
    falling = 1.0 - scaled * scaled
    envelope = falling * falling
    orders = (rows_of((NBASIS, PAIRS)) + 1).astype(F32)
    sine, cosine = sin_cos_half_turns(orders * scaled)
    over = sine * inverse
    radial = over * envelope
    r8 = rows_of((8, PAIRS)).astype(F32)
    own_kind = own_rows[3] - 1.0
    near_kind = near_rows[3] - 1.0
    one_hots = jnp.where(
        r8 < NSPEC,
        jnp.where(r8 == own_kind, 1.0, 0.0),
        jnp.where(r8 - NSPEC == near_kind, jnp.where(r8 < 2 * NSPEC, 1.0, 0.0), 0.0),
    )
    features = jnp.concatenate(
        [radial, one_hots, jnp.zeros((BLK - 16, PAIRS), F32)], axis=0
    ).astype(BF16)

    y4 = jnp.concatenate([jnp.ones_like(distance)] + way, axis=0)
    y_high, y_low = halves(y4)
    none = jnp.zeros_like(y_high)
    products = dot_tn(
        jnp.concatenate([y_high, y_high, y_low, none], axis=0).astype(F32),
        jnp.concatenate([y_high, y_low, y_high, none], axis=0).astype(F32),
    )
    g_matrix = (same[...] * products).astype(BF16)

    spans = [slice(j * CHUNK, (j + 1) * CHUNK) for j in range(CHUNKS)]

    for s in spans:
        value, slope = silu_parts(dot(w_in[...], features[:, s]))
        d1[:, s] = slope
        value, slope = silu_parts(dot(w_hidden[...], value.astype(BF16)))
        d2[:, s] = slope
        h2[:, s] = value
        latent[:, s] = value * envelope[:, s]
    for l in range(2):
        for j, s in enumerate(spans):
            half = latent[:, s].astype(BF16)
            env_w[l, :, s] = dot(w_env[l], half) * live[:, s]
            inners[:, s] = half
        weights_half = env_w[l].astype(BF16)
        for j, s in enumerate(spans):
            gathered = dot(weights_half, g_matrix[:, s])
            env_a[l, :, s] = gathered
            invariant = (0.5 * env_w[l, :, s] * gathered).astype(BF16)
            value, slope = silu_parts(
                dot(w_latent[l], jnp.concatenate([inners[:, s], invariant, no_rows], axis=0))
            )
            dz[l, :, s] = slope
            latent[:, s] = latent[:, s] + value
    for l in range(2):
        stacked_a[l * MULT : (l + 1) * MULT, :] = env_w[l]
        stacked_b[(2 + l) * MULT : (3 + l) * MULT, :] = env_w[l].astype(BF16)
    left[:, : 2 * MULT] = jnp.transpose(stacked_a[: 2 * MULT], (1, 0)).astype(BF16)

    for l in (1, 0):
        for s in spans:
            inner = (grad[:, s] * dz[l, :, s]).astype(BF16)
            inners[:, s] = inner
            d_invariant = 0.5 * dot(w_latent_t[l, CH:], inner)
            stacked_a[(2 + l) * MULT : (3 + l) * MULT, s] = d_invariant * env_w[l, :, s]
            env_a[l, :, s] = d_invariant * env_a[l, :, s]
        d_gathered = stacked_a[(2 + l) * MULT : (3 + l) * MULT, :].astype(BF16)
        stacked_b[l * MULT : (l + 1) * MULT, :] = d_gathered
        if l == 0:
            left[:, 2 * MULT :] = jnp.transpose(stacked_a[2 * MULT :], (1, 0)).astype(BF16)
            d_products = (same[...] * dot(left[...], stacked_b[...])).astype(BF16)
            d_y = dot(y_high, d_products)
            d_way = [d_y[1 + c : 2 + c] for c in range(3)]
        for s in spans:
            d_weights = (env_a[l, :, s] + dot(d_gathered, g_matrix[:, s])) * live[:, s]
            both = jnp.concatenate([inners[:, s], d_weights.astype(BF16), no_rows], axis=0)
            grad[:, s] = grad[:, s] + dot(w_back[l], both)
    d_radial = []
    d_envelope = []
    for s in spans:
        d_latent = grad[:, s]
        d_envelope.append(jnp.sum(d_latent * h2[:, s], axis=0, keepdims=True))
        inner = (d_latent * envelope[:, s] * d2[:, s]).astype(BF16)
        inner = (dot(w_hidden_t[...], inner) * d1[:, s]).astype(BF16)
        d_radial.append(dot(w_in_t[...], inner)[:NBASIS])
    d_radial = jnp.concatenate(d_radial, axis=1)
    d_envelope = jnp.concatenate(d_envelope, axis=1)

    slope_envelope = falling * scaled * (-4.0 / CUTOFF)
    d_envelope = d_envelope + jnp.sum(d_radial * over, axis=0, keepdims=True)
    d_over = d_radial * envelope
    turning = cosine * orders * (3.14159265358979 / CUTOFF) - over
    d_distance = (
        d_envelope * slope_envelope
        + inverse * jnp.sum(d_over * turning, axis=0, keepdims=True)
        - inverse * (d_way[0] * way[0] + d_way[1] * way[1] + d_way[2] * way[2])
    )
    gradient = [d_way[c] * inverse + d_distance * way[c] for c in range(3)]

    def scattered(count, values, hot, block_index):
        pattern = jnp.concatenate(values + [jnp.zeros((1, PAIRS), F32)], axis=0)
        pattern = jnp.concatenate([pattern, pattern], axis=0)
        pattern = jnp.broadcast_to(pattern[None], (count // 2, 8, PAIRS)).reshape(4 * count, PAIRS)
        spread = jnp.where(rows_of((4 * count, PAIRS)) >> 2 == block_index, pattern, 0.0)
        return dot_nt(spread.astype(BF16), hot).reshape(count, 4, BLK)

    partial[...] = scattered(PADDED, [-g for g in gradient], lane_neighbour[:BLK], block)
    for offset in near:
        a, b, c = offset
        at = 9 * (a + 1) + 3 * (b + 1) + (c + 1)
        pltpu.make_async_remote_copy(
            src_ref=partial.at[pl.ds(6 * at, 6)],
            dst_ref=arrived.at[pl.ds(6 * at, 6)],
            send_sem=back_send_sem,
            recv_sem=back_recv_sem,
            device_id=device(offset),
            device_id_type=MESH,
        ).start()
    arrived[6 * 13 : 6 * 14] = partial[6 * 13 : 6 * 14]
    own_part = scattered(8, gradient, lane_centre[:BLK], centre_block)
    energy = jnp.zeros((1, 1), F32)
    for s in spans:
        values = dot(out_row, latent[:, s].astype(BF16))
        energy = energy + jnp.sum(values * live[:, s], axis=1, keepdims=True)
    results[0, 0, 3, :, :BLK] = jnp.broadcast_to(energy, (1, BLK))

    pltpu.make_async_copy(
        arrived.at[pl.ds(0, 6 * 26)], arrived.at[pl.ds(0, 6 * 26)], back_recv_sem
    ).wait()
    for s in range(6):
        total = own_part[s]
        for o in range(27):
            total = total + arrived[6 * o + s]
        for c in range(3):
            results[0, 0, c, :, s * BLK : (s + 1) * BLK] = total[c : c + 1]

    results[0, 0, 3, :, BLK:] = jnp.zeros((1, 5 * BLK), F32)

    pltpu.make_async_copy(
        held.at[pl.ds(0, incoming)], held.at[pl.ds(0, incoming)], send_sem
    ).wait()
    pltpu.make_async_copy(
        partial.at[pl.ds(0, 6 * 26)], partial.at[pl.ds(0, 6 * 26)], back_send_sem
    ).wait()


def hand_over(results, forces, energy):
    forces[...] = results[:, :, :3]
    energy[0] = results[0, 0, 3, :, 0:1]


def on_device(sizes, positions, *arrays):
    *arrays, w_in, w_hidden, w_env, w_latent, w_out = arrays
    vmem = pltpu.VMEM
    results = pl.pallas_call(
        functools.partial(kernel, sizes),
        out_shape=jax.ShapeDtypeStruct((1, 1, 4, 1, 6 * BLK), F32),
        in_specs=[pl.BlockSpec(memory_space=pltpu.HBM)] * 5
        + [pl.BlockSpec(memory_space=pltpu.SMEM)]
        + [pl.BlockSpec(memory_space=pltpu.HBM)] * 5,
        out_specs=pl.BlockSpec(memory_space=vmem),
        scratch_shapes=[
            vmem((3, 1, NB * BLK), F32),
            vmem((1, NB * BLK), jnp.int32),
            pltpu.SMEM((1, NB), jnp.int32),
            vmem((1, PAIRS), jnp.int32),
            vmem((1, PAIRS), jnp.int32),
            pltpu.SMEM((1, 1), jnp.int32),
            vmem((NBASIS + 2 * NSPEC, CH), BF16),
            vmem((CH, CH), BF16),
            vmem((2, MULT, CH), BF16),
            vmem((2, CH + MULT, CH), BF16),
            vmem((2, CH // 2), BF16),
            vmem((16, CH), BF16),
            vmem((CH, BLK), BF16),
            vmem((CH, CH), BF16),
            vmem((2, CH, CH + BLK), BF16),
            vmem((2, CH, CH + BLK), BF16),
            vmem((6, 4, BLK), F32),
            vmem((PADDED, 4, BLK), F32),
            vmem((2 * BLK, PAIRS), BF16),
            vmem((2 * BLK, PAIRS), BF16),
            vmem((PAIRS, PAIRS), F32),
            vmem((CH, PAIRS), F32),
            vmem((CH, PAIRS), F32),
            vmem((CH, PAIRS), F32),
            vmem((CH, PAIRS), F32),
            vmem((CH, PAIRS), F32),
            vmem((CH, PAIRS), BF16),
            vmem((2, CH, PAIRS), F32),
            vmem((2, MULT, PAIRS), F32),
            vmem((2, MULT, PAIRS), F32),
            vmem((4 * MULT, PAIRS), F32),
            vmem((4 * MULT, PAIRS), BF16),
            vmem((PAIRS, 4 * MULT), BF16),
            vmem((PADDED, 4, BLK), F32),
            vmem((6 * 27, 4, BLK), F32),
            pltpu.SemaphoreType.DMA((11,)),
            pltpu.SemaphoreType.DMA,
            pltpu.SemaphoreType.DMA,
            pltpu.SemaphoreType.DMA,
            pltpu.SemaphoreType.DMA,
        ],
        compiler_params=pltpu.CompilerParams(
            collective_id=0, has_side_effects=True, vmem_limit_bytes=63 * 1024 * 1024
        ),
        cost_estimate=pl.CostEstimate(flops=10**9, bytes_accessed=10**6, transcendentals=10**6),
    )(
        positions.transpose(0, 1, 3, 2, 4),
        *arrays,
        w_in.T,
        w_hidden,
        w_env,
        w_latent.transpose(0, 2, 1),
        w_out.reshape(2, CH // 2),
    )
    forces, energy = pl.pallas_call(
        hand_over,
        out_shape=(
            jax.ShapeDtypeStruct((1, 1, 3, 1, 6 * BLK), F32),
            jax.ShapeDtypeStruct((1, 1, 1), F32),
        ),
        in_specs=(pl.BlockSpec(memory_space=vmem),),
        out_specs=(pl.BlockSpec(memory_space=vmem),) * 2,
        compiler_params=pltpu.CompilerParams(vmem_limit_bytes=63 * 1024 * 1024),
    )(results)
    return forces.transpose(0, 1, 3, 2, 4), energy


def solution(mesh):
    sizes = tuple(mesh.shape[axis] for axis in ("gx", "gy", "gz"))
    return jax.shard_map(
        functools.partial(on_device, sizes),
        mesh=mesh,
        in_specs=(
            P("gx", "gy", "gz", None, None),
            P("gx", "gy", "gz", None),
            P("gx", "gy", "gz", None),
            P("gx", "gy", "gz", None),
            P("gx", "gy", "gz", None),
            P("gx", "gy", "gz"),
            P(),
            P(),
            P(),
            P(),
            P(),
        ),
        out_specs=(P("gx", "gy", "gz", None, None), P("gx", "gy", "gz")),
        check_vma=False,
    )
```

```python
import functools

import jax
import jax.numpy as jnp
from jax import lax
from jax.experimental import pallas as pl
from jax.experimental.pallas import tpu as pltpu
from jax.sharding import PartitionSpec as P

MESH = pl.DeviceIdType.MESH

CH = 256
MULT = 64
NBASIS = 8
NSPEC = 3
BLK = 128
NB = 4
PAIRS = 512
CHUNK = 256
CHUNKS = PAIRS // CHUNK

EDGE = 1.5
CUTOFF = 9.0
SOFT2 = 0.25

GROUP = 18
FIRST = {-2: 0, -1: 1, 0: 6, 1: 12, 2: 17}
SENT = {-2: (5, 1), -1: (1, 5), 0: (0, 6), 1: (0, 5), 2: (0, 1)}
ROWS = 9 * GROUP
PADDED = 164
OWN = 4 * GROUP + FIRST[0]

F32 = jnp.float32
BF16 = jnp.bfloat16


def dot(a, b):
    return lax.dot_general(a, b, (((1,), (0,)), ((), ())), preferred_element_type=F32)


def dot_tn(a, b):
    return lax.dot_general(a, b, (((0,), (0,)), ((), ())), preferred_element_type=F32)


def dot_nt(a, b):
    return lax.dot_general(a, b, (((1,), (1,)), ((), ())), preferred_element_type=F32)


def halves(x):
    high = x.astype(BF16)
    return high, (x - high.astype(F32)).astype(BF16)


def rows_of(shape):
    return lax.broadcasted_iota(jnp.int32, shape, 0)


def series(u, terms):
    total = jnp.full_like(u, terms[-1])
    for term in terms[-2::-1]:
        total = total * u + term
    return total


def sin_cos_half_turns(t):
    k = jnp.floor(t + 0.5)
    f = (t - k) * 3.14159265358979
    sign = 1.0 - 2.0 * (k - 2.0 * jnp.floor(0.5 * k))
    u = f * f
    sine = f * series(u, [1.0, -1 / 6, 1 / 120, -1 / 5040, 1 / 362880, -1 / 39916800, 1 / 6227020800])
    cosine = series(
        u, [1.0, -1 / 2, 1 / 24, -1 / 720, 1 / 40320, -1 / 3628800, 1 / 479001600, -1 / 87178291200]
    )
    return sign * sine, sign * cosine


def silu_parts(x):
    gate = 0.5 + 0.5 * jnp.tanh(0.5 * x)
    value = x * gate
    return value, gate + value * (1.0 - gate)


def kernel(
    sizes,
    pos_hbm, kind_hbm, plan_hbm, centre_hbm, neighbour_hbm, blocks_hbm,
    w_in_hbm, w_hidden_hbm, w_env_hbm, w_latent_hbm, w_out_hbm,
    results,
    pos, kind, plan, centre, neighbour, blocks,
    w_in_raw, w_hidden, w_env, w_latent_t, w_out,
    w_in_t, w_in, w_hidden_t, w_back, w_latent,
    mine, held, lane_neighbour, lane_centre, same,
    d1, d2, h2, latent, grad, inners, dz, env_w, env_a, stacked_a, stacked_b, left,
    partial, arrived,
    in_sems, send_sem, recv_sem, back_send_sem, back_recv_sem,
):
    place = [lax.axis_index(axis) for axis in ("gx", "gy", "gz")]

    def device(steps):
        return tuple(
            lax.rem(at + (step + size), size) if step else at
            for at, step, size in zip(place, steps, sizes)
        )

    far = [(a, b, c) for b in (-1, 0, 1) for c in (-1, 0, 1) for a in (-2, -1, 0, 1, 2)]
    far = [o for o in far if o != (0, 0, 0)]
    far.sort(key=lambda o: -(2 * (abs(o[1]) + abs(o[2])) + abs(o[0])))
    far = [x for o in far if o > (0, 0, 0) for x in (o, (-o[0], -o[1], -o[2]))]
    near = [o for o in far if abs(o[0]) < 2]

    pairs_in = [
        (pos_hbm.at[0, 0], pos),
        (kind_hbm.at[0, 0], kind),
        (plan_hbm.at[0, 0], plan),
        (centre_hbm.at[0, 0], centre),
        (neighbour_hbm.at[0, 0], neighbour),
        (w_in_hbm, w_in_raw),
        (w_hidden_hbm, w_hidden),
        (w_env_hbm, w_env),
        (w_latent_hbm, w_latent_t),
        (w_out_hbm, w_out),
    ]
    loads = [
        pltpu.make_async_copy(source, target, in_sems.at[i])
        for i, (source, target) in enumerate(pairs_in)
    ]
    for load in loads:
        load.start()

    barrier = pltpu.get_barrier_semaphore()
    for offset in far:
        pl.semaphore_signal(barrier, inc=1, device_id=device(offset), device_id_type=MESH)

    for load in loads[:3]:
        load.wait()
    kind_rows = kind[...].astype(F32) + 1.0
    for b in range(NB):
        lanes_of = slice(b * BLK, (b + 1) * BLK)
        for c in range(3):
            mine[1 + b, c : c + 1] = pos[c, :, lanes_of]
        mine[1 + b, 3:4] = kind_rows[:, lanes_of]
    first_row = (rows_of((4, BLK)) == 0).astype(F32)
    for slot, move, shift in ((0, 1, -EDGE), (5, 2, EDGE)):
        packed = jnp.zeros((4, BLK), F32)
        for b in range(NB):
            chosen = jnp.where(plan[0, b] == move, 1.0, 0.0).astype(F32)
            packed = packed + chosen * (mine[1 + b] + shift * first_row)
        mine[slot] = packed
    held[OWN : OWN + 6] = mine[...]
    held[ROWS:] = jnp.zeros((PADDED - ROWS, 4, BLK), F32)

    pl.semaphore_wait(barrier, len(far))
    for offset in far:
        a, b, c = offset
        start, count = SENT[a]
        where = (3 * (1 - b) + (1 - c)) * GROUP + FIRST[-a]
        pltpu.make_async_remote_copy(
            src_ref=mine.at[pl.ds(start, count)],
            dst_ref=held.at[pl.ds(where, count)],
            send_sem=send_sem,
            recv_sem=recv_sem,
            device_id=device(offset),
            device_id_type=MESH,
        ).start()

    for load in loads[3:]:
        load.wait()
    centre_row = centre[...]
    neighbour_row = neighbour[...]
    live = jnp.where(
        lax.broadcasted_iota(jnp.int32, (1, PAIRS), 1) < blocks_hbm[0, 0, 0] * BLK, 1.0, 0.0
    ).astype(F32)
    centre_block = centre_row >> 7
    centre_lane = centre_row & 127
    block = neighbour_row >> 7
    neighbour_lane = neighbour_row & 127
    box = (block * 10923) >> 16
    k = block - 6 * box
    box_x = (box * 7282) >> 16
    box_yz = box - 9 * box_x
    box_y = (box_yz * 21846) >> 16
    box_z = box_yz - 3 * box_y

    def held_row(x, yz, k):
        up = jnp.where(x == 2, 6, x)
        down = jnp.where(x == 0, 11, 15 + x)
        return yz * GROUP + jnp.where(k == 0, up, jnp.where(k == 5, down, 1 + 5 * x + k))

    neighbour_held = held_row(box_x, box_yz, k)
    centre_held = held_row(jnp.ones_like(centre_block), jnp.zeros_like(centre_block), centre_block)
    home = jnp.zeros_like(box)
    for at, (a, b, c) in enumerate(near + [(0, 0, 0)]):
        home = home + jnp.where(box == 9 * (a + 1) + 3 * (b + 1) + (c + 1), at, 0)
    neighbour_home = 6 * home + k
    lanes = rows_of((BLK, PAIRS))
    hot = jnp.where(lanes == neighbour_lane, 1.0, 0.0).astype(BF16)
    lane_neighbour[:BLK] = hot
    lane_neighbour[BLK:] = hot
    hot = jnp.where(lanes == centre_lane, 1.0, 0.0).astype(BF16)
    lane_centre[:BLK] = hot
    lane_centre[BLK:] = hot
    centre_column = jnp.transpose(
        jnp.broadcast_to(centre_row.astype(F32), (8, PAIRS)), (1, 0)
    )[:, 0:1]
    same[...] = jnp.where(centre_column == centre_row.astype(F32), 1.0, 0.0).astype(F32)

    w_hidden_t[...] = jnp.transpose(w_hidden[...].astype(F32), (1, 0)).astype(BF16)
    for l in range(2):
        padding = jnp.zeros((BLK - MULT, CH), F32)
        rows = jnp.concatenate([w_env[l].astype(F32), padding], axis=0)
        w_back[l, :, :CH] = w_latent_t[l, :CH]
        w_back[l, :, CH:] = jnp.transpose(rows, (1, 0)).astype(BF16)
        rows = jnp.concatenate([w_latent_t[l].astype(F32), padding], axis=0)
        w_latent[l] = jnp.transpose(rows, (1, 0)).astype(BF16)
    fewer = NBASIS + 2 * NSPEC
    rows = jnp.concatenate([w_in_raw[...].astype(F32), jnp.zeros((BLK - fewer, CH), F32)], axis=0)
    w_in_t[...] = rows[:16].astype(BF16)
    w_in[...] = jnp.transpose(rows, (1, 0)).astype(BF16)
    no_rows = jnp.zeros((BLK - MULT, CHUNK), BF16)
    out_row = jnp.concatenate([w_out[0:1], w_out[1:2]], axis=1)
    out_column = jnp.transpose(jnp.broadcast_to(out_row.astype(F32), (8, CH)), (1, 0))[:, 0:1]
    grad[...] = out_column * live

    incoming = ROWS - 6
    pltpu.make_async_copy(
        held.at[pl.ds(0, incoming)], held.at[pl.ds(0, incoming)], recv_sem
    ).wait()

    def found_at(table, hot, block_index):
        count = table.shape[0] * 4
        high, low = halves(table.reshape(count, BLK))
        found = dot(jnp.concatenate([high, low], axis=1), hot)
        found = jnp.where(rows_of((count, PAIRS)) >> 2 == block_index, found, 0.0)
        found = jnp.sum(found.reshape(count // 8, 8, PAIRS), axis=0)
        found = found[0:4] + found[4:8]
        return [found[c : c + 1] for c in range(4)]

    near_rows = found_at(held[...], lane_neighbour[...], neighbour_held)
    own_rows = found_at(held[4 * GROUP : 4 * GROUP + 20], lane_centre[...], centre_held)

    shifts = [EDGE * (v.astype(F32) - 1.0) for v in (box_x, box_y, box_z)]
    gap = [near_rows[c] + shifts[c] - own_rows[c] for c in range(3)]
    square = gap[0] * gap[0] + gap[1] * gap[1] + gap[2] * gap[2]
    inverse = lax.rsqrt(square + SOFT2)
    distance = (square + SOFT2) * inverse
    way = [g * inverse for g in gap]
    scaled = distance * (1.0 / CUTOFF)
    falling = 1.0 - scaled * scaled
    envelope = falling * falling
    orders = (rows_of((NBASIS, PAIRS)) + 1).astype(F32)
    sine, cosine = sin_cos_half_turns(orders * scaled)
    over = sine * inverse
    radial = over * envelope
    r8 = rows_of((8, PAIRS)).astype(F32)
    own_kind = own_rows[3] - 1.0
    near_kind = near_rows[3] - 1.0
    one_hots = jnp.where(
        r8 < NSPEC,
        jnp.where(r8 == own_kind, 1.0, 0.0),
        jnp.where(r8 - NSPEC == near_kind, jnp.where(r8 < 2 * NSPEC, 1.0, 0.0), 0.0),
    )
    features = jnp.concatenate(
        [radial, one_hots, jnp.zeros((BLK - 16, PAIRS), F32)], axis=0
    ).astype(BF16)

    y4 = jnp.concatenate([jnp.ones_like(distance)] + way, axis=0)
    y_high, y_low = halves(y4)
    none = jnp.zeros_like(y_high)
    products = dot_tn(
        jnp.concatenate([y_high, y_high, y_low, none], axis=0).astype(F32),
        jnp.concatenate([y_high, y_low, y_high, none], axis=0).astype(F32),
    )
    g_matrix = (same[...] * products).astype(BF16)

    spans = [slice(j * CHUNK, (j + 1) * CHUNK) for j in range(CHUNKS)]

    for s in spans:
        value, slope = silu_parts(dot(w_in[...], features[:, s]))
        d1[:, s] = slope
        value, slope = silu_parts(dot(w_hidden[...], value.astype(BF16)))
        d2[:, s] = slope
        h2[:, s] = value
        latent[:, s] = value * envelope[:, s]
    for l in range(2):
        for j, s in enumerate(spans):
            half = latent[:, s].astype(BF16)
            env_w[l, :, s] = dot(w_env[l], half) * live[:, s]
            inners[:, s] = half
        weights_half = env_w[l].astype(BF16)
        for j, s in enumerate(spans):
            gathered = dot(weights_half, g_matrix[:, s])
            env_a[l, :, s] = gathered
            invariant = (0.5 * env_w[l, :, s] * gathered).astype(BF16)
            value, slope = silu_parts(
                dot(w_latent[l], jnp.concatenate([inners[:, s], invariant, no_rows], axis=0))
            )
            dz[l, :, s] = slope
            latent[:, s] = latent[:, s] + value
    for l in range(2):
        stacked_a[l * MULT : (l + 1) * MULT, :] = env_w[l]
        stacked_b[(2 + l) * MULT : (3 + l) * MULT, :] = env_w[l].astype(BF16)
    left[:, : 2 * MULT] = jnp.transpose(stacked_a[: 2 * MULT], (1, 0)).astype(BF16)

    for l in (1, 0):
        for s in spans:
            inner = (grad[:, s] * dz[l, :, s]).astype(BF16)
            inners[:, s] = inner
            d_invariant = 0.5 * dot(w_latent_t[l, CH:], inner)
            stacked_a[(2 + l) * MULT : (3 + l) * MULT, s] = d_invariant * env_w[l, :, s]
            env_a[l, :, s] = d_invariant * env_a[l, :, s]
        d_gathered = stacked_a[(2 + l) * MULT : (3 + l) * MULT, :].astype(BF16)
        stacked_b[l * MULT : (l + 1) * MULT, :] = d_gathered
        if l == 0:
            left[:, 2 * MULT :] = jnp.transpose(stacked_a[2 * MULT :], (1, 0)).astype(BF16)
            d_products = (same[...] * dot(left[...], stacked_b[...])).astype(BF16)
            d_y = dot(y_high, d_products)
            d_way = [d_y[1 + c : 2 + c] for c in range(3)]
        for s in spans:
            d_weights = (env_a[l, :, s] + dot(d_gathered, g_matrix[:, s])) * live[:, s]
            both = jnp.concatenate([inners[:, s], d_weights.astype(BF16), no_rows], axis=0)
            grad[:, s] = grad[:, s] + dot(w_back[l], both)
    d_radial = []
    d_envelope = []
    for s in spans:
        d_latent = grad[:, s]
        d_envelope.append(jnp.sum(d_latent * h2[:, s], axis=0, keepdims=True))
        inner = (d_latent * envelope[:, s] * d2[:, s]).astype(BF16)
        inner = (dot(w_hidden_t[...], inner) * d1[:, s]).astype(BF16)
        d_radial.append(dot(w_in_t[...], inner)[:NBASIS])
    d_radial = jnp.concatenate(d_radial, axis=1)
    d_envelope = jnp.concatenate(d_envelope, axis=1)

    slope_envelope = falling * scaled * (-4.0 / CUTOFF)
    d_envelope = d_envelope + jnp.sum(d_radial * over, axis=0, keepdims=True)
    d_over = d_radial * envelope
    turning = cosine * orders * (3.14159265358979 / CUTOFF) - over
    d_distance = (
        d_envelope * slope_envelope
        + inverse * jnp.sum(d_over * turning, axis=0, keepdims=True)
        - inverse * (d_way[0] * way[0] + d_way[1] * way[1] + d_way[2] * way[2])
    )
    gradient = [d_way[c] * inverse + d_distance * way[c] for c in range(3)]

    def scattered(count, values, hot, block_index):
        pattern = jnp.concatenate(values + [jnp.zeros((1, PAIRS), F32)], axis=0)
        pattern = jnp.concatenate([pattern, pattern], axis=0)
        pattern = jnp.broadcast_to(pattern[None], (count // 2, 8, PAIRS)).reshape(4 * count, PAIRS)
        spread = jnp.where(rows_of((4 * count, PAIRS)) >> 2 == block_index, pattern, 0.0)
        return dot_nt(spread.astype(BF16), hot).reshape(count, 4, BLK)

    def send_back(places):
        for at in places:
            offset = near[at]
            pltpu.make_async_remote_copy(
                src_ref=partial.at[pl.ds(6 * at, 6)],
                dst_ref=arrived.at[pl.ds(6 * at, 6)],
                send_sem=back_send_sem,
                recv_sem=back_recv_sem,
                device_id=device(offset),
                device_id_type=MESH,
            ).start()

    negative = [-g for g in gradient]
    for first, last in ((0, 14), (14, 27)):
        count = 6 * (last - first)
        padded = count + count % 4
        partial[6 * first : 6 * first + padded] = scattered(
            padded, negative, lane_neighbour[:BLK], neighbour_home - 6 * first
        )
        send_back(range(first, min(last, 26)))
    arrived[6 * 26 : 6 * 27] = partial[6 * 26 : 6 * 27]
    own_part = scattered(8, gradient, lane_centre[:BLK], centre_block)
    energy = jnp.zeros((1, 1), F32)
    for s in spans:
        values = dot(out_row, latent[:, s].astype(BF16))
        energy = energy + jnp.sum(values * live[:, s], axis=1, keepdims=True)
    results[0, 0, 3, :, :BLK] = jnp.broadcast_to(energy, (1, BLK))

    pltpu.make_async_copy(
        arrived.at[pl.ds(0, 6 * 26)], arrived.at[pl.ds(0, 6 * 26)], back_recv_sem
    ).wait()
    for s in range(6):
        total = own_part[s]
        for o in range(27):
            total = total + arrived[6 * o + s]
        for c in range(3):
            results[0, 0, c, :, s * BLK : (s + 1) * BLK] = total[c : c + 1]

    results[0, 0, 3, :, BLK:] = jnp.zeros((1, 5 * BLK), F32)

    pltpu.make_async_copy(
        held.at[pl.ds(0, incoming)], held.at[pl.ds(0, incoming)], send_sem
    ).wait()
    pltpu.make_async_copy(
        partial.at[pl.ds(0, 6 * 26)], partial.at[pl.ds(0, 6 * 26)], back_send_sem
    ).wait()


def hand_over(results, forces, energy):
    forces[...] = results[:, :, :3]
    energy[0] = results[0, 0, 3, :, 0:1]


def on_device(sizes, positions, *arrays):
    *arrays, w_in, w_hidden, w_env, w_latent, w_out = arrays
    vmem = pltpu.VMEM
    results = pl.pallas_call(
        functools.partial(kernel, sizes),
        out_shape=jax.ShapeDtypeStruct((1, 1, 4, 1, 6 * BLK), F32),
        in_specs=[pl.BlockSpec(memory_space=pltpu.HBM)] * 5
        + [pl.BlockSpec(memory_space=pltpu.SMEM)]
        + [pl.BlockSpec(memory_space=pltpu.HBM)] * 5,
        out_specs=pl.BlockSpec(memory_space=vmem),
        scratch_shapes=[
            vmem((3, 1, NB * BLK), F32),
            vmem((1, NB * BLK), jnp.int32),
            pltpu.SMEM((1, NB), jnp.int32),
            vmem((1, PAIRS), jnp.int32),
            vmem((1, PAIRS), jnp.int32),
            pltpu.SMEM((1, 1), jnp.int32),
            vmem((NBASIS + 2 * NSPEC, CH), BF16),
            vmem((CH, CH), BF16),
            vmem((2, MULT, CH), BF16),
            vmem((2, CH + MULT, CH), BF16),
            vmem((2, CH // 2), BF16),
            vmem((16, CH), BF16),
            vmem((CH, BLK), BF16),
            vmem((CH, CH), BF16),
            vmem((2, CH, CH + BLK), BF16),
            vmem((2, CH, CH + BLK), BF16),
            vmem((6, 4, BLK), F32),
            vmem((PADDED, 4, BLK), F32),
            vmem((2 * BLK, PAIRS), BF16),
            vmem((2 * BLK, PAIRS), BF16),
            vmem((PAIRS, PAIRS), F32),
            vmem((CH, PAIRS), F32),
            vmem((CH, PAIRS), F32),
            vmem((CH, PAIRS), F32),
            vmem((CH, PAIRS), F32),
            vmem((CH, PAIRS), F32),
            vmem((CH, PAIRS), BF16),
            vmem((2, CH, PAIRS), F32),
            vmem((2, MULT, PAIRS), F32),
            vmem((2, MULT, PAIRS), F32),
            vmem((4 * MULT, PAIRS), F32),
            vmem((4 * MULT, PAIRS), BF16),
            vmem((PAIRS, 4 * MULT), BF16),
            vmem((PADDED, 4, BLK), F32),
            vmem((6 * 27, 4, BLK), F32),
            pltpu.SemaphoreType.DMA((11,)),
            pltpu.SemaphoreType.DMA,
            pltpu.SemaphoreType.DMA,
            pltpu.SemaphoreType.DMA,
            pltpu.SemaphoreType.DMA,
        ],
        compiler_params=pltpu.CompilerParams(
            collective_id=0, has_side_effects=True, vmem_limit_bytes=63 * 1024 * 1024
        ),
        cost_estimate=pl.CostEstimate(flops=10**9, bytes_accessed=10**6, transcendentals=10**6),
    )(
        positions.transpose(0, 1, 3, 2, 4),
        *arrays,
        w_in.T,
        w_hidden,
        w_env,
        w_latent.transpose(0, 2, 1),
        w_out.reshape(2, CH // 2),
    )
    forces, energy = pl.pallas_call(
        hand_over,
        out_shape=(
            jax.ShapeDtypeStruct((1, 1, 3, 1, 6 * BLK), F32),
            jax.ShapeDtypeStruct((1, 1, 1), F32),
        ),
        in_specs=(pl.BlockSpec(memory_space=vmem),),
        out_specs=(pl.BlockSpec(memory_space=vmem),) * 2,
        compiler_params=pltpu.CompilerParams(vmem_limit_bytes=63 * 1024 * 1024),
    )(results)
    return forces.transpose(0, 1, 3, 2, 4), energy


def solution(mesh):
    sizes = tuple(mesh.shape[axis] for axis in ("gx", "gy", "gz"))
    return jax.shard_map(
        functools.partial(on_device, sizes),
        mesh=mesh,
        in_specs=(
            P("gx", "gy", "gz", None, None),
            P("gx", "gy", "gz", None),
            P("gx", "gy", "gz", None),
            P("gx", "gy", "gz", None),
            P("gx", "gy", "gz", None),
            P("gx", "gy", "gz"),
            P(),
            P(),
            P(),
            P(),
            P(),
        ),
        out_specs=(P("gx", "gy", "gz", None, None), P("gx", "gy", "gz")),
        check_vma=False,
    )
```
